256 devices in a mesh: expert: 32 (over z, y), seq: 4 (over x), dp: 2 (over core).
Axes of the slice: x: 4, y: 4, z: 8, core: 2. Of those that a mesh axis runs over, the one named last changes fastest.
Arguments:
- hidden_in: bfloat16 [32768, 2048], P(('expert', 'seq', 'dp')), may hold values from -20 to 20
- norm_gain: float32 [2048], replicated, may hold values from 0.5 to 1.5
- router_weight: bfloat16 [2048, 64], replicated, may hold values from -0.125 to 0.125
- routes: int32 [32768, 6], P(('expert', 'seq', 'dp')), may hold values from 0 to 63, all different within a row; in each aligned block of 128 rows (0 to 127, 128 to 255, ...) at most 13 rows name the same one
- w_gate: bfloat16 [64, 2048, 1408], P(('expert', 'dp'), 'seq'), may hold values from -0.125 to 0.125
- w_up: bfloat16 [64, 2048, 1408], P(('expert', 'dp'), 'seq'), may hold values from -0.125 to 0.125
- w_down: bfloat16 [64, 1408, 2048], P(('expert', 'dp'), 'seq'), may hold values from -0.15625 to 0.15625
- cached_layers: bfloat16 [3, 32768, 2048], P(None, ('expert', 'seq', 'dp')), may hold values from -40 to 40
- student_hidden: bfloat16 [32768, 2048], P(('expert', 'seq', 'dp')), may hold values from -24 to 24
- prediction: bfloat16 [32768, 1024], P(('expert', 'seq', 'dp')), may hold values from -6 to 6
Outputs:
- targets: bfloat16 [32768, 2048], P(('expert', 'seq', 'dp'))
- head_grad: float32 [2048, 1024], P(('expert', 'seq', 'dp'))
The draws below stay inside these ranges and needn't reach their ends.
Inputs may be any that keep to these rules, and one draw needn't show every extreme that they name: `routes`: each row names 6 different experts. Among the 128 rows of one device no expert is named more than 13 times, a bound that some block reaches.
All inputs are finite; a program needn't handle non-finite values.
Results may differ from the reference program's by a relative error of at most 0.0025.
The reference program's roundings to bfloat16 on the way count: a program that leaves them out, or rounds other values in their place, can miss the bound.
Values may be sent and summed in bfloat16 or wider, within the bound.
A program may use at most 128 MiB of HBM per device.

```python
import math
import jax
import jax.numpy as jnp
import numpy as np
from jax import lax

D = 2048
FF = 1408
TOP = 6
AVG = 4
DW = 1024
TOK_DEV = 128
EXPERTS = 64
CAP = 13
TOKENS = 32768


def trended(key, noise, spread):
    first, second = jax.random.split(key)
    count = noise.shape[0]
    position = jnp.arange(TOKENS, dtype=jnp.float32) / TOKENS
    ramp = 1.0 + 2.0 * position
    levels = jax.random.uniform(first, (count, 1, D), jnp.float32, -1.5, 1.5)
    scales = jnp.exp(jax.random.uniform(second, (count, 1, D), jnp.float32, 0.0, spread))
    return levels * ramp[None, :, None] + noise * scales * (0.5 + 0.5 * ramp)[None, :, None]


def draw_hidden_in(key, part):
    key = jax.random.fold_in(key, 3)
    noise_key, other_key = jax.random.split(key)
    noise = jnp.clip(jax.random.normal(noise_key, (1, TOKENS, D), jnp.float32), -5.0, 5.0)
    values = trended(other_key, noise, 0.7)
    return (0.5 * values[0]).astype(jnp.bfloat16)


def draw_cached_layers(key, part):
    key = jax.random.fold_in(key, 11)
    noise_key, other_key = jax.random.split(key)
    noise = jnp.clip(jax.random.normal(noise_key, (AVG - 1, TOKENS, D), jnp.float32), -5.0, 5.0)
    values = trended(other_key, noise, 0.7)
    return values.astype(jnp.bfloat16)


def with_spikes(values, stream_key, source, target, blocks, factor):
    owner, partner = [(jnp.arange(values.shape[dim]) // (values.shape[dim] // blocks)).reshape([-1 if axis == dim else 1 for axis in range(values.ndim)]) for dim in (source, target)]
    chosen = jax.random.permutation(stream_key, blocks)[partner]
    strong = (owner == chosen) | (owner == (partner + blocks // 2) % blocks)
    return jnp.where(strong, factor * values, values)


def level_of(own_key, shape, cuts, least, top_value):
    level, own = 1.0, jax.random.fold_in(own_key, 6)
    for dim, shards_of in cuts:
        heights = jnp.exp(jax.random.uniform(jax.random.fold_in(own, dim), (shards_of,), jnp.float32, least / len(cuts), top_value / len(cuts)))
        level = level * jnp.repeat(heights, shape[dim] // shards_of).reshape([-1 if axis == dim else 1 for axis in range(len(shape))])
    return level


def deal_out(key, own, number, rows, amount, top, limit, skew):
    ranking = jax.random.permutation(key, amount)
    heavy_load, usual = portions_of(amount, rows * top, limit, skew, True), portions_of(amount, rows * top, limit, skew, False)
    places = jnp.arange(amount)

    def named(sizes, rotation):
        used = int((sizes > 0).sum())
        fixed = max(1, used // 4)
        passed = fixed + (places - fixed + rotation * (used - fixed)) % max(1, amount - fixed)
        return jnp.zeros((amount,), jnp.int32).at[ranking[jnp.where(places < fixed, places, passed)]].set(jnp.asarray(sizes, jnp.int32))

    sizes = jnp.where(number % 4 == 0, named(heavy_load, number // 4), named(usual, number - number // 4 - 1))
    mixed = jax.random.permutation(jax.random.fold_in(own, 3), amount)
    donor, sink = mixed[0:amount // 2 * 2:2], mixed[1:amount // 2 * 2:2]
    margin = jnp.minimum(sizes[donor] - 1, limit - sizes[sink]) // 2
    margin = jnp.where((donor == ranking[0]) | (sink == ranking[0]) | (sizes[sink] == 0), 0, jnp.maximum(margin, 0))
    passed = jax.random.randint(jax.random.fold_in(own, 4), (amount // 2,), 0, 1 << 20) % (margin + 1)
    sizes = sizes.at[donor].add(-passed).at[sink].add(passed)
    members = jnp.searchsorted(jnp.cumsum(sizes), jnp.arange(rows * top), side="right").astype(jnp.int32)
    table = members.reshape(top, rows).T
    table = table[jax.random.permutation(jax.random.fold_in(own, 1), rows)]
    rotation = jax.random.randint(jax.random.fold_in(own, 2), (rows, 1), 0, top)
    return jnp.take_along_axis(table, (jnp.arange(top)[None, :] + rotation) % top, axis=1)


def portions_of(amount, total, limit, skew, full):
    portions = [(1 << 20) // math.isqrt(grade ** skew) + 1 for grade in range(1, amount + 1)]
    largest = limit if full else min(limit, max(-(-total // amount), total * portions[0] // sum(portions)))
    least = 1 if total - largest >= amount - 1 else 0
    given, surplus = [largest] + [least] * (amount - 1), total - largest - least * (amount - 1)
    while surplus > 0:
        free = [i for i in range(1, amount) if given[i] < largest] or [i for i in range(1, amount) if given[i] < limit]
        pool, remaining = sum([portions[i] for i in free]), surplus
        for i in free:
            more = min(limit - given[i], max(1, remaining * portions[i] // pool), surplus)
            given[i] = given[i] + more
            surplus = surplus - more
    return np.array(given)


def bell_draw(own_key, extent, deviation, bound, cuts=(), kind=jnp.bfloat16):
    values = deviation * jax.random.normal(own_key, extent, jnp.float32)
    if cuts:
        values = values * level_of(own_key, extent, cuts, -0.22, 0.18)
    return jnp.clip(values, -bound, bound).astype(kind)


def heavy_noise(rng, shape, deviation, bound, shards, heavy, kind=jnp.bfloat16):
    drawn = deviation * jax.random.normal(rng, shape, jnp.float32)
    if shards:
        drawn = drawn * level_of(rng, shape, shards, -0.22, 0.18)
    return jnp.clip(with_spikes(drawn, jax.random.fold_in(rng, 3), *heavy), -bound, bound).astype(kind)


def setup_inputs(seed: int = 0) -> dict:
    streams_of = jax.random.split(jax.random.key(seed), 11)
    hidden_in = draw_hidden_in(jax.random.fold_in(streams_of[10], 71), 0)
    norm_gain = jnp.clip(jax.random.uniform(streams_of[1], (D,), jnp.float32, 0.5, 1.5), 0.5, 1.5)
    router_weight = bell_draw(streams_of[2], (D, EXPERTS), D ** -0.5, 0.125)
    routes_keys = jax.random.split(jax.random.fold_in(streams_of[3], 1), TOKENS // TOK_DEV)
    routes_turns = jax.random.permutation(jax.random.fold_in(streams_of[3], 3), TOKENS // TOK_DEV)
    routes = jax.vmap(lambda own, number: deal_out(jax.random.fold_in(streams_of[3], 2), own, number, TOK_DEV, EXPERTS, TOP, CAP, 2))(routes_keys, routes_turns).reshape((TOKENS, TOP))
    w_gate = bell_draw(streams_of[4], (EXPERTS, D, FF), D ** -0.5, 0.125, ((0, 64), (1, 4)))
    w_up = bell_draw(streams_of[5], (EXPERTS, D, FF), D ** -0.5, 0.125, ((0, 64), (1, 4)))
    w_down = bell_draw(streams_of[6], (EXPERTS, FF, D), FF ** -0.5, 0.15625, ((0, 64), (1, 4)))
    cached_layers = draw_cached_layers(jax.random.fold_in(streams_of[10], 71), 0)
    student_hidden = heavy_noise(streams_of[8], (TOKENS, D), 1.0, 24.0, ((0, 256),), (0, 1, 256, 6.0))
    prediction = bell_draw(streams_of[9], (TOKENS, DW), 1.0, 6.0, ((0, 256),))
    return {"hidden_in": hidden_in, "norm_gain": norm_gain, "router_weight": router_weight, "routes": routes, "w_gate": w_gate, "w_up": w_up, "w_down": w_down, "cached_layers": cached_layers, "student_hidden": student_hidden, "prediction": prediction}


def reference(hidden_in, norm_gain, router_weight, routes, w_gate, w_up, w_down, cached_layers, student_hidden, prediction):
    hidden32 = hidden_in.astype(jnp.float32)
    normed = (hidden32 * lax.rsqrt(lax.optimization_barrier(jnp.mean(hidden32 * hidden32, axis=-1, keepdims=True)) + 1e-06) * norm_gain).astype(jnp.bfloat16)
    logits = jnp.dot(normed, router_weight, preferred_element_type=jnp.float32)
    picked = routes[:, :, None] == jnp.arange(EXPERTS, dtype=jnp.int32)[None, None, :]
    chosen = lax.optimization_barrier(jnp.sum(jnp.where(picked, logits[:, None, :], jnp.zeros((), jnp.float32)), axis=-1))
    affinity = jax.nn.sigmoid(chosen)
    gate_share = affinity / lax.optimization_barrier(jnp.sum(affinity, axis=-1, keepdims=True))
    blocks = TOKENS // TOK_DEV
    flags = picked.reshape(blocks, TOK_DEV * TOP, EXPERTS).astype(jnp.int32)
    running = jnp.cumsum(flags, axis=1)
    slot_index = (lax.optimization_barrier(jnp.sum(running * flags, axis=-1)) - 1).reshape(TOKENS * TOP).astype(jnp.int32)
    pair_ids = jnp.arange(TOKENS * TOP, dtype=jnp.int32)
    block_of = pair_ids // (TOK_DEV * TOP)
    token_of = pair_ids // TOP
    flat_routes = routes.reshape(-1).astype(jnp.int32)
    flat_gates = gate_share.reshape(-1)
    rows_per = blocks * CAP
    padded = jnp.concatenate([normed, jnp.zeros((1, D), jnp.bfloat16)], axis=0)

    def one_expert(mixture, expert):
        place = jnp.where(flat_routes == expert, block_of * CAP + slot_index, rows_per).astype(jnp.int32)
        source_row = jnp.full((rows_per,), TOKENS, jnp.int32).at[place].set(token_of, mode='drop')
        weights_row = jnp.zeros((rows_per,), jnp.float32).at[place].set(flat_gates, mode='drop')
        expert_rows = padded[source_row]
        gate_acc = jnp.dot(expert_rows, w_gate[expert], preferred_element_type=jnp.float32)
        up_acc = jnp.dot(expert_rows, w_up[expert], preferred_element_type=jnp.float32)
        activation = (jax.nn.silu(gate_acc) * up_acc).astype(jnp.bfloat16)
        expert_out = jnp.dot(activation, w_down[expert], preferred_element_type=jnp.float32).astype(jnp.bfloat16)
        contrib = weights_row[:, None] * expert_out.astype(jnp.float32)
        mixture = mixture.at[source_row].add(contrib, mode='drop')
        return (mixture, None)
    mixture, _ = lax.scan(one_expert, jnp.zeros((TOKENS, D), jnp.float32), jnp.arange(EXPERTS, dtype=jnp.int32))
    layer_out = hidden32 + mixture
    summed = jnp.zeros((TOKENS, D), jnp.float32)
    for layer in range(AVG):
        values = cached_layers[layer].astype(jnp.float32) if layer < AVG - 1 else layer_out
        means = lax.optimization_barrier(jnp.sum(values, axis=0)) / TOKENS
        variance = lax.optimization_barrier(jnp.sum(values * values, axis=0)) / TOKENS - means * means
        summed = summed + (values - means[None, :]) * lax.rsqrt(variance + 1e-05)[None, :]
    targets = (summed / AVG).astype(jnp.bfloat16)
    scale = 1.0 / math.sqrt(TOKENS)
    residual = ((prediction.astype(jnp.float32) - targets[:, :DW].astype(jnp.float32)) * scale).astype(jnp.bfloat16)
    head_grad = lax.dot_general(student_hidden, residual, (((0,), (0,)), ((), ())), preferred_element_type=jnp.float32)
    return (targets, head_grad)
```

```python
import functools
import math

import jax
import jax.numpy as jnp
from jax import lax
from jax.experimental import pallas as pl
from jax.experimental.pallas import tpu as pltpu
from jax.sharding import PartitionSpec as P

MESH = pl.DeviceIdType.MESH
F32, BF16 = jnp.float32, jnp.bfloat16
NY = 4


def wheel():
    e, x, c = lax.axis_index("expert"), lax.axis_index("seq"), lax.axis_index("dp")
    nz = lax.axis_size("expert") // NY
    z, y = e // NY, lax.rem(e, NY)

    def to(z_, y_, x_, c_):
        return {"expert": z_ * NY + y_, "seq": x_, "dp": c_}

    return {
        "c": (c, 2, lambda d: to(z, y, x, lax.rem(c + d, 2))),
        "x": (x, lax.axis_size("seq"), lambda d: to(z, y, lax.rem(x + d, lax.axis_size("seq")), c)),
        "y": (y, NY, lambda d: to(z, lax.rem(y + d, NY), x, c)),
        "z": (z, nz, lambda d: to(lax.rem(z + d, nz), y, x, c)),
    }


def start_all(axis, source, target, send, recv):
    _, n, device = axis
    copies = []
    for d in range(1, n):
        copy = pltpu.make_async_remote_copy(
            src_ref=source(d),
            dst_ref=target(d),
            send_sem=send.at[d - 1],
            recv_sem=recv.at[d - 1],
            device_id=device(d),
            device_id_type=MESH,
        )
        copy.start()
        copies.append(copy)
    return copies


def wait_all(copies):
    for copy in copies:
        copy.wait()


def fold(row_list):
    w = row_list[0].shape[1] // 4
    return jnp.concatenate([r[:, i * w : (i + 1) * w] for r in row_list for i in range(4)], axis=0)


def unfold(block, row):
    return jnp.concatenate([block[4 * row + i : 4 * row + i + 1, :] for i in range(4)], axis=1)


def column_sums(values):
    return [jnp.sum(values, axis=0, keepdims=True), jnp.sum(values * values, axis=0, keepdims=True)]


def tail_kernel(
    total_tokens,
    back_ref,
    mix_ref,
    hidden_ref,
    cached_ref,
    prediction_ref,
    student_ref,
    targets_ref,
    grad_ref,
    layer_out,
    stat_own,
    stat_c,
    stat_x,
    stat_y,
    stat_z,
    students,
    residuals,
    partial,
    from_c,
    from_y,
    from_z,
    sem_st,
    sem_s,
    sem_x,
    sem_c,
    sem_y,
    sem_z,
):
    axes = wheel()
    tok, width = hidden_ref.shape
    window = prediction_ref.shape[1]
    x = axes["x"][0]
    c = axes["c"][0]

    barrier = pltpu.get_barrier_semaphore()
    greeted = 0
    for name in "cxyz":
        _, n, device = axes[name]
        for d in range(1, n):
            pl.semaphore_signal(barrier, inc=1, device_id=device(d), device_id_type=MESH)
            greeted += 1
    pl.semaphore_wait(barrier, greeted)

    nx = axes["x"][1]
    students_out = start_all(
        axes["x"],
        lambda d: student_ref.at[lax.rem(x + d, nx)],
        lambda d: students.at[d],
        sem_st.at[0],
        sem_st.at[1],
    )

    stats = []
    for layer in range(3):
        stats += column_sums(cached_ref[layer].astype(F32))
    cut = 512
    for j in range(width // cut):
        cols = slice(j * cut, (j + 1) * cut)
        both = jnp.dot(mix_ref[...], back_ref[:, cols], preferred_element_type=F32)
        layer_out[:, cols] = hidden_ref[:, cols].astype(F32) + (both[:tok] + both[tok:])
    stats += column_sums(layer_out[...])
    stat_own[0] = fold(stats)
    for i, (name, slots) in enumerate((("c", stat_c), ("x", stat_x), ("y", stat_y), ("z", stat_z))):
        copies = start_all(
            axes[name],
            lambda d, i=i: stat_own.at[i],
            lambda d, slots=slots: slots.at[d - 1],
            sem_s.at[i, 0],
            sem_s.at[i, 1],
        )
        for copy in copies:
            copy.wait_recv()
        total = stat_own[i]
        for d in range(1, axes[name][1]):
            total = total + slots[d - 1]
        stat_own[i + 1] = total
        for copy in copies:
            copy.wait_send()
    total = stat_own[4]
    for j in range(width // cut):
        cols = slice(j * cut, (j + 1) * cut)
        summed = jnp.zeros((tok, cut), F32)
        for layer in range(4):
            mean = total[8 * layer + j : 8 * layer + j + 1, :] / total_tokens
            square = total[8 * layer + 4 + j : 8 * layer + 5 + j, :] / total_tokens
            inverse = lax.rsqrt(square - mean * mean + 1e-5)
            values = cached_ref[layer, :, cols].astype(F32) if layer < 3 else layer_out[:, cols]
            summed = summed + (values - mean) * inverse
        targets = (summed * 0.25).astype(BF16)
        targets_ref[:, cols] = targets
        if (j + 1) * cut <= window:
            scale = 1.0 / math.sqrt(total_tokens)
            residuals[0, :, cols] = (
                (prediction_ref[:, cols].astype(F32) - targets.astype(F32)) * scale
            ).astype(BF16)

    copies = start_all(
        axes["x"],
        lambda d: residuals.at[0],
        lambda d: residuals.at[d],
        sem_x.at[0],
        sem_x.at[1],
    )
    for copy in students_out:
        copy.wait()
    students[0] = student_ref[x]
    rows = partial.shape[0]
    half = rows // 2
    for d in range(nx):
        if d:
            copies[d - 1].wait_recv()

        def add(i, _):
            at = pl.ds(pl.multiple_of(i * 128, 128), 128)
            product = jnp.dot(students[d, at, :], residuals[d], preferred_element_type=F32)
            partial[at, :] = product if d == 0 else partial[at, :] + product
            return _

        lax.fori_loop(0, rows // 128, add, 0)
    for copy in copies:
        copy.wait_send()
    other = pl.ds(pl.multiple_of((1 - c) * half, half), half)
    mine = pl.ds(pl.multiple_of(c * half, half), half)
    wait_all(
        start_all(
            axes["c"],
            lambda d: partial.at[other],
            lambda d: from_c,
            sem_c.at[0],
            sem_c.at[1],
        )
    )
    from_c[...] = from_c[...] + partial[mine, :]
    y, ny, _ = axes["y"]
    part = half // ny

    def y_rows(d):
        return pl.ds(pl.multiple_of(lax.rem(y + d, ny) * part, part), part)

    wait_all(
        start_all(
            axes["y"],
            lambda d: from_c.at[y_rows(d)],
            lambda d: from_y.at[d],
            sem_y.at[0],
            sem_y.at[1],
        )
    )
    total = from_c[y_rows(0), :]
    for d in range(1, ny):
        total = total + from_y[d]
    from_y[0] = total
    z, nz, _ = axes["z"]
    least = part // nz

    def z_rows(d):
        return pl.ds(pl.multiple_of(lax.rem(z + d, nz) * least, least), least)

    wait_all(
        start_all(
            axes["z"],
            lambda d: from_y.at[0, z_rows(d)],
            lambda d: from_z.at[d],
            sem_z.at[0],
            sem_z.at[1],
        )
    )
    total = from_y[0, z_rows(0), :]
    for d in range(1, nz):
        total = total + from_z[d]
    grad_ref[...] = total


def tail(total_tokens, back, mix, hidden_in, cached, prediction, student):
    tok, width = hidden_in.shape
    window = prediction.shape[1]
    nx, ny, nz = lax.axis_size("seq"), NY, lax.axis_size("expert") // NY
    rows = width // nx
    vmem = pl.BlockSpec(memory_space=pltpu.VMEM)
    dma = pltpu.SemaphoreType.DMA
    stat = (32, width // 4)
    return pl.pallas_call(
        functools.partial(tail_kernel, total_tokens),
        out_shape=(
            jax.ShapeDtypeStruct((tok, width), BF16),
            jax.ShapeDtypeStruct((rows // (2 * ny * nz), window), F32),
        ),
        in_specs=[vmem] * 6,
        out_specs=(vmem, vmem),
        scratch_shapes=[
            pltpu.VMEM((tok, width), F32),
            pltpu.VMEM((5, *stat), F32),
            pltpu.VMEM((1, *stat), F32),
            pltpu.VMEM((nx - 1, *stat), F32),
            pltpu.VMEM((ny - 1, *stat), F32),
            pltpu.VMEM((nz - 1, *stat), F32),
            pltpu.VMEM((nx, rows, tok), BF16),
            pltpu.VMEM((nx, tok, window), BF16),
            pltpu.VMEM((rows, window), F32),
            pltpu.VMEM((rows // 2, window), F32),
            pltpu.VMEM((ny, rows // (2 * ny), window), F32),
            pltpu.VMEM((nz, rows // (2 * ny * nz), window), F32),
            dma((2, nx - 1)),
            dma((4, 2, 7)),
            dma((2, nx - 1)),
            dma((2, 1)),
            dma((2, ny - 1)),
            dma((2, nz - 1)),
        ],
        compiler_params=pltpu.CompilerParams(
            collective_id=1, has_side_effects=True, vmem_limit_bytes=40 * 2**20
        ),
    )(back, mix, hidden_in, cached, prediction, student)


SLOTS = 16


def body(
    hidden_in,
    norm_gain,
    router_weight,
    routes,
    w_gate,
    w_up,
    w_down,
    cached_layers,
    student_hidden,
    prediction,
):
    tok, width = hidden_in.shape
    n_experts = router_weight.shape[1]
    nx, nz = lax.axis_size("seq"), lax.axis_size("expert") // NY
    total_tokens = tok * lax.axis_size(("expert", "seq", "dp"))
    hidden32 = hidden_in.astype(F32)
    normed = (
        hidden32
        * lax.rsqrt(jnp.mean(hidden32 * hidden32, axis=-1, keepdims=True) + 1e-06)
        * norm_gain
    ).astype(BF16)
    logits = jnp.dot(normed, router_weight, preferred_element_type=F32)
    picked = jnp.any(routes[:, :, None] == jnp.arange(n_experts, dtype=jnp.int32), axis=1)
    earlier = jnp.tril(jnp.ones((tok, tok), BF16), -1)
    place = jnp.dot(earlier, picked.astype(BF16), preferred_element_type=F32)
    affinity = jnp.where(picked, jax.nn.sigmoid(logits), 0.0)
    share = affinity / jnp.sum(affinity, axis=-1, keepdims=True)
    slots = jnp.arange(SLOTS, dtype=F32)
    where = picked[:, :, None] & (place[:, :, None] == slots)
    pick = where.reshape(tok, n_experts * SLOTS).astype(BF16)
    mix = jnp.where(where, share[:, :, None], 0.0).reshape(tok, n_experts * SLOTS)
    high = mix.astype(BF16)
    low = (mix - high.astype(F32)).astype(BF16)
    mix = jnp.concatenate([high, low], axis=0)
    outgoing = lax.dot_general(
        pick, normed, (((0,), (0,)), ((), ())), preferred_element_type=F32
    ).astype(BF16)

    def exchange(rows):
        return lax.all_to_all(
            rows.reshape(n_experts, SLOTS, width),
            ("expert", "dp"),
            split_axis=0,
            concat_axis=0,
            tiled=True,
        ).reshape(n_experts * SLOTS, width)

    rows = exchange(outgoing)
    gate_acc = jnp.dot(
        rows, lax.all_gather(w_gate[0], "seq", axis=0, tiled=True), preferred_element_type=F32
    )
    up_acc = jnp.dot(
        rows, lax.all_gather(w_up[0], "seq", axis=0, tiled=True), preferred_element_type=F32
    )
    activation = (jax.nn.silu(gate_acc) * up_acc).astype(BF16)
    expert_out = jnp.dot(
        activation,
        lax.all_gather(w_down[0], "seq", axis=0, tiled=True),
        preferred_element_type=F32,
    ).astype(BF16)
    back = exchange(expert_out)
    student = (
        student_hidden.T.reshape(nz, NY, nx, 2, width // (2 * nx * NY * nz), tok)
        .transpose(2, 3, 1, 0, 4, 5)
        .reshape(nx, width // nx, tok)
    )
    return tail(total_tokens, back, mix, hidden_in, cached_layers, prediction, student)


def solution(mesh):
    tokens = P(("expert", "seq", "dp"), None)
    weights = P(("expert", "dp"), "seq", None)
    return jax.shard_map(
        body,
        mesh=mesh,
        in_specs=(
            tokens,
            P(),
            P(),
            tokens,
            weights,
            weights,
            weights,
            P(None, ("expert", "seq", "dp"), None),
            tokens,
            tokens,
        ),
        out_specs=(tokens, tokens),
        check_vma=False,
    )
```

```python
import functools
import math

import jax
import jax.numpy as jnp
from jax import lax
from jax.experimental import pallas as pl
from jax.experimental.pallas import tpu as pltpu
from jax.sharding import PartitionSpec as P

MESH = pl.DeviceIdType.MESH
F32, BF16 = jnp.float32, jnp.bfloat16
NY = 4


def wheel():
    e, x, c = lax.axis_index("expert"), lax.axis_index("seq"), lax.axis_index("dp")
    nz = lax.axis_size("expert") // NY
    z, y = e // NY, lax.rem(e, NY)

    def to(z_, y_, x_, c_):
        return {"expert": z_ * NY + y_, "seq": x_, "dp": c_}

    return {
        "c": (c, 2, lambda d: to(z, y, x, lax.rem(c + d, 2))),
        "x": (x, lax.axis_size("seq"), lambda d: to(z, y, lax.rem(x + d, lax.axis_size("seq")), c)),
        "y": (y, NY, lambda d: to(z, lax.rem(y + d, NY), x, c)),
        "z": (z, nz, lambda d: to(lax.rem(z + d, nz), y, x, c)),
    }


def start_all(axis, source, target, send, recv):
    _, n, device = axis
    copies = []
    for d in range(1, n):
        copy = pltpu.make_async_remote_copy(
            src_ref=source(d),
            dst_ref=target(d),
            send_sem=send.at[d - 1],
            recv_sem=recv.at[d - 1],
            device_id=device(d),
            device_id_type=MESH,
        )
        copy.start()
        copies.append(copy)
    return copies


def wait_all(copies):
    for copy in copies:
        copy.wait()


def fold(row_list):
    w = row_list[0].shape[1] // 4
    return jnp.concatenate([r[:, i * w : (i + 1) * w] for r in row_list for i in range(4)], axis=0)


def unfold(block, row):
    return jnp.concatenate([block[4 * row + i : 4 * row + i + 1, :] for i in range(4)], axis=1)


def column_sums(values):
    return [jnp.sum(values, axis=0, keepdims=True), jnp.sum(values * values, axis=0, keepdims=True)]


SLOTS = 16
CHUNK = 512
TILE = 256


def kernel(
    total_tokens,
    outgoing_ref,
    mix_ref,
    hidden_ref,
    cached_ref,
    prediction_ref,
    student_ref,
    wg_ref,
    wu_ref,
    wd_ref,
    targets_ref,
    grad_ref,
    wg,
    wu,
    wd,
    arrived,
    act,
    out,
    back,
    layer_out,
    cached_own,
    cached_c,
    cached_x,
    cached_y,
    cached_z,
    stat_own,
    stat_c,
    stat_x,
    stat_y,
    stat_z,
    students,
    residuals,
    partial,
    from_c,
    from_y,
    from_z,
    sem_own,
    sem_w,
    sem_rows,
    sem_back,
    sem_st,
    sem_s,
    sem_x,
    sem_c,
    sem_y,
    sem_z,
):
    axes = wheel()
    tok, width = hidden_ref.shape
    window = prediction_ref.shape[1]
    e, x, c = lax.axis_index("expert"), lax.axis_index("seq"), lax.axis_index("dp")
    nx = axes["x"][1]
    n = 2 * lax.axis_size("expert")
    me = 2 * e + c
    half = width // 2

    def peer(d):
        p = lax.rem(me + d, n)
        return p, {"expert": p // 2, "seq": x, "dp": lax.rem(p, 2)}

    barrier = pltpu.get_barrier_semaphore()

    def greet(d, _):
        pl.semaphore_signal(barrier, inc=1, device_id=peer(d)[1], device_id_type=MESH)
        return _

    lax.fori_loop(1, n, greet, 0)
    for d in range(1, nx):
        pl.semaphore_signal(barrier, inc=1, device_id=axes["x"][2](d), device_id_type=MESH)
    pl.semaphore_wait(barrier, n - 1 + nx - 1)

    right, left = axes["x"][2](1), axes["x"][2](nx - 1)
    before, after = lax.rem(x + nx - 1, nx), lax.rem(x + 1, nx)

    def weight_piece(number, shard, whole, cols):
        rows = shard.shape[0]
        cut = rows // 2

        def at(origin, part):
            return pl.ds(pl.multiple_of(origin * rows + part * cut, 16), cut)

        def copy(i, source, origin, part, device):
            return pltpu.make_async_remote_copy(
                src_ref=source,
                dst_ref=whole.at[at(origin, part), cols],
                send_sem=sem_w.at[number, 0, i],
                recv_sem=sem_w.at[number, 1, i],
                device_id=device,
                device_id_type=MESH,
            )

        def own(part):
            return shard.at[pl.ds(part * cut, cut), cols]

        def passed(origin, part):
            return whole.at[at(origin, part), cols]

        return [
            copy(0, own(0), x, 0, right),
            copy(1, own(1), x, 1, right),
            copy(2, own(1), x, 1, left),
            copy(3, own(0), x, 0, left),
            copy(4, passed(before, 0), before, 0, right),
            copy(5, passed(after, 1), after, 1, left),
        ]

    def begin(piece):
        for i in (0, 2, 1, 3):
            piece[i].start()

    def pass_on(piece):
        piece[0].wait_recv()
        piece[4].start()
        piece[2].wait_recv()
        piece[5].start()

    every = slice(0, wg.shape[1])
    gate_piece = weight_piece(0, wg_ref, wg, every)
    up_piece = weight_piece(1, wu_ref, wu, every)
    down_pieces = [weight_piece(2 + i, wd_ref, wd, slice(i * half, (i + 1) * half)) for i in range(2)]
    begin(gate_piece)

    def block(p):
        return pl.ds(pl.multiple_of(p * SLOTS, SLOTS), SLOTS)

    def scatter(source, target, send, recv):
        def go(d, _):
            p, device = peer(d)
            pltpu.make_async_remote_copy(
                src_ref=source.at[block(p)],
                dst_ref=target.at[block(me)],
                send_sem=send,
                recv_sem=recv,
                device_id=device,
                device_id_type=MESH,
            ).start()
            return _

        lax.fori_loop(1, n, go, 0)
        target[block(me), :] = source[block(me), :]

    def wait_rows(ref, sem):
        rows = ref.at[pl.ds(0, (n - 1) * SLOTS)]
        pltpu.make_async_copy(rows, rows, sem).wait()

    scatter(outgoing_ref, arrived, sem_rows.at[0], sem_rows.at[1])
    mine = []
    for i, (shard, whole) in enumerate(((wg_ref, wg), (wu_ref, wu), (wd_ref, wd))):
        rows = shard.shape[0]
        copy = pltpu.make_async_copy(
            shard, whole.at[pl.ds(pl.multiple_of(x * rows, 16), rows)], sem_own.at[i]
        )
        copy.start()
        mine.append(copy)
    students_out = start_all(
        axes["x"],
        lambda d: student_ref.at[lax.rem(x + d, nx)],
        lambda d: students.at[d],
        sem_st.at[0],
        sem_st.at[1],
    )
    students[0] = student_ref[x]

    def add_over_devices(number, own, slots):
        for i, name in enumerate("cxyz"):
            copies = start_all(
                axes[name],
                lambda d: own.at[i],
                lambda d: slots[i].at[d - 1],
                sem_s.at[number, i, 0],
                sem_s.at[number, i, 1],
            )
            wait_all(copies)
            total = own[i]
            for d in range(1, axes[name][1]):
                total = total + slots[i][d - 1]
            own[i + 1] = total

    stats = []
    for layer in range(3):
        stats += column_sums(cached_ref[layer].astype(F32))
    cached_own[0] = fold(stats)

    pass_on(gate_piece)
    gate_piece[1].wait_recv()
    gate_piece[3].wait_recv()
    begin(up_piece)
    add_over_devices(0, cached_own, (cached_c, cached_x, cached_y, cached_z))
    pass_on(up_piece)
    gate_piece[4].wait_recv()
    gate_piece[5].wait_recv()
    up_piece[1].wait_recv()
    up_piece[3].wait_recv()
    begin(down_pieces[0])
    up_piece[4].wait_recv()
    up_piece[5].wait_recv()
    for copy in mine:
        copy.wait()
    wait_rows(arrived, sem_rows.at[1])

    def activate(i, _):
        at = pl.ds(pl.multiple_of(i * TILE, TILE), TILE)
        gate = jnp.dot(arrived[at, :], wg[...], preferred_element_type=F32)
        up = jnp.dot(arrived[at, :], wu[...], preferred_element_type=F32)
        act[at, :] = (gate * jax.nn.sigmoid(gate) * up).astype(BF16)
        return _

    tiles = arrived.shape[0] // TILE
    lax.fori_loop(0, tiles // 2, activate, 0)
    pass_on(down_pieces[0])
    lax.fori_loop(tiles // 2, tiles, activate, 0)
    down_pieces[0][1].wait_recv()
    down_pieces[0][3].wait_recv()
    begin(down_pieces[1])
    down_pieces[0][4].wait_recv()
    down_pieces[0][5].wait_recv()

    chunks = width // CHUNK
    for j in range(chunks):
        if j == chunks // 2:
            for i in (1, 3, 4, 5):
                down_pieces[1][i].wait_recv()

        def project(i, _):
            at = pl.ds(pl.multiple_of(i * TILE, TILE), TILE)
            out[j, at, :] = jnp.dot(
                act[at, :], wd[:, j * CHUNK : (j + 1) * CHUNK], preferred_element_type=F32
            ).astype(BF16)
            return _

        lax.fori_loop(0, tiles, project, 0)
        scatter(out.at[j], back.at[j], sem_back.at[0, j], sem_back.at[1, j])
        if j == chunks // 2 - 1:
            pass_on(down_pieces[1])

    scale = 1.0 / math.sqrt(total_tokens)
    tail_cut = 4

    def finish(h):
        for j in range(h * chunks // 2, (h + 1) * chunks // 2):
            wait_rows(back.at[j], sem_back.at[1, j])
            cols = slice(j * CHUNK, (j + 1) * CHUNK)
            both = jnp.dot(mix_ref[...], back[j], preferred_element_type=F32)
            layer_out[:, cols] = hidden_ref[:, cols].astype(F32) + (both[:tok] + both[tok:])
        stat_own[h, 0] = fold(column_sums(layer_out[:, h * half : (h + 1) * half]))
        slots = [s.at[h] for s in (stat_c, stat_x, stat_y, stat_z)]
        add_over_devices(1 + h, stat_own.at[h], slots)
        last = stat_own[h, 4]
        earlier = cached_own[4]
        w = half // tail_cut
        for j in range(h * chunks // 2, (h + 1) * chunks // 2):
            cols = slice(j * CHUNK, (j + 1) * CHUNK)
            summed = jnp.zeros((tok, CHUNK), F32)
            for layer in range(4):
                if layer < 3:
                    sums = earlier[8 * layer + j : 8 * layer + j + 1, :]
                    squares = earlier[8 * layer + 4 + j : 8 * layer + 5 + j, :]
                    values = cached_ref[layer, :, cols].astype(F32)
                else:
                    k = (j - h * chunks // 2) * (CHUNK // w)
                    sums = jnp.concatenate([last[k : k + 1], last[k + 1 : k + 2]], axis=1)
                    squares = jnp.concatenate([last[4 + k : 5 + k], last[5 + k : 6 + k]], axis=1)
                    values = layer_out[:, cols]
                mean = sums / total_tokens
                variance = squares / total_tokens - mean * mean
                summed = summed + (values - mean) * lax.rsqrt(variance + 1e-5)
            targets = (summed * 0.25).astype(BF16)
            targets_ref[:, cols] = targets
            if (j + 1) * CHUNK <= window:
                residuals[0, :, cols] = (
                    (prediction_ref[:, cols].astype(F32) - targets.astype(F32)) * scale
                ).astype(BF16)

    finish(0)
    copies = start_all(
        axes["x"],
        lambda d: residuals.at[0],
        lambda d: residuals.at[d],
        sem_x.at[0],
        sem_x.at[1],
    )
    wait_all(students_out)
    rows = partial.shape[0]
    halved = rows // 2
    for d in range(nx):
        if d:
            copies[d - 1].wait_recv()

        def add(i, _):
            at = pl.ds(pl.multiple_of(i * 128, 128), 128)
            product = jnp.dot(students[d, at, :], residuals[d], preferred_element_type=F32)
            partial[at, :] = product if d == 0 else partial[at, :] + product
            return _

        lax.fori_loop(0, rows // 128, add, 0)
    for copy in copies:
        copy.wait_send()
    other = pl.ds(pl.multiple_of((1 - c) * halved, halved), halved)
    kept = pl.ds(pl.multiple_of(c * halved, halved), halved)
    wait_all(
        start_all(
            axes["c"],
            lambda d: partial.at[other],
            lambda d: from_c,
            sem_c.at[0],
            sem_c.at[1],
        )
    )
    from_c[...] = from_c[...] + partial[kept, :]
    y, ny, _ = axes["y"]
    part = halved // ny

    def y_rows(d):
        return pl.ds(pl.multiple_of(lax.rem(y + d, ny) * part, part), part)

    wait_all(
        start_all(
            axes["y"],
            lambda d: from_c.at[y_rows(d)],
            lambda d: from_y.at[d],
            sem_y.at[0],
            sem_y.at[1],
        )
    )
    total = from_c[y_rows(0), :]
    for d in range(1, ny):
        total = total + from_y[d]
    from_y[0] = total
    z, nz, _ = axes["z"]
    least = part // nz

    def z_rows(d):
        return pl.ds(pl.multiple_of(lax.rem(z + d, nz) * least, least), least)

    wait_all(
        start_all(
            axes["z"],
            lambda d: from_y.at[0, z_rows(d)],
            lambda d: from_z.at[d],
            sem_z.at[0],
            sem_z.at[1],
        )
    )
    total = from_y[0, z_rows(0), :]
    for d in range(1, nz):
        total = total + from_z[d]
    grad_ref[...] = total

    finish(1)
    for piece in (gate_piece, up_piece, *down_pieces):
        for copy in piece:
            copy.wait_send()
    wait_rows(outgoing_ref, sem_rows.at[0])
    for j in range(chunks):
        wait_rows(out.at[j], sem_back.at[0, j])


def run(total_tokens, outgoing, mix, hidden_in, cached, prediction, student, wg, wu, wd):
    tok, width = hidden_in.shape
    window = prediction.shape[1]
    nx, ny, nz = lax.axis_size("seq"), NY, lax.axis_size("expert") // NY
    rows = width // nx
    hidden_units = wg.shape[1]
    arrived = outgoing.shape[0]
    chunks = width // CHUNK
    vmem = pl.BlockSpec(memory_space=pltpu.VMEM)
    hbm = pl.BlockSpec(memory_space=pl.ANY)
    dma = pltpu.SemaphoreType.DMA
    early, late = (24, width // 4), (8, width // 8)
    return pl.pallas_call(
        functools.partial(kernel, total_tokens),
        out_shape=(
            jax.ShapeDtypeStruct((tok, width), BF16),
            jax.ShapeDtypeStruct((rows // (2 * ny * nz), window), F32),
        ),
        in_specs=[vmem] * 6 + [hbm] * 3,
        out_specs=(vmem, vmem),
        scratch_shapes=[
            pltpu.VMEM((width, hidden_units), BF16),
            pltpu.VMEM((width, hidden_units), BF16),
            pltpu.VMEM((hidden_units, width), BF16),
            pltpu.VMEM((arrived, width), BF16),
            pltpu.VMEM((arrived, hidden_units), BF16),
            pltpu.VMEM((chunks, arrived, CHUNK), BF16),
            pltpu.VMEM((chunks, arrived, CHUNK), BF16),
            pltpu.VMEM((tok, width), F32),
            pltpu.VMEM((5, *early), F32),
            pltpu.VMEM((1, *early), F32),
            pltpu.VMEM((nx - 1, *early), F32),
            pltpu.VMEM((ny - 1, *early), F32),
            pltpu.VMEM((nz - 1, *early), F32),
            pltpu.VMEM((2, 5, *late), F32),
            pltpu.VMEM((2, 1, *late), F32),
            pltpu.VMEM((2, nx - 1, *late), F32),
            pltpu.VMEM((2, ny - 1, *late), F32),
            pltpu.VMEM((2, nz - 1, *late), F32),
            pltpu.VMEM((nx, rows, tok), BF16),
            pltpu.VMEM((nx, tok, window), BF16),
            pltpu.VMEM((rows, window), F32),
            pltpu.VMEM((rows // 2, window), F32),
            pltpu.VMEM((ny, rows // (2 * ny), window), F32),
            pltpu.VMEM((nz, rows // (2 * ny * nz), window), F32),
            dma((3,)),
            dma((4, 2, 6)),
            dma((2,)),
            dma((2, chunks)),
            dma((2, nx - 1)),
            dma((3, 4, 2, 7)),
            dma((2, nx - 1)),
            dma((2, 1)),
            dma((2, ny - 1)),
            dma((2, nz - 1)),
        ],
        compiler_params=pltpu.CompilerParams(
            collective_id=1, has_side_effects=True, vmem_limit_bytes=60 * 2**20
        ),
    )(outgoing, mix, hidden_in, cached, prediction, student, wg, wu, wd)


def body(
    hidden_in,
    norm_gain,
    router_weight,
    routes,
    w_gate,
    w_up,
    w_down,
    cached_layers,
    student_hidden,
    prediction,
):
    tok, width = hidden_in.shape
    n_experts = router_weight.shape[1]
    nx, nz = lax.axis_size("seq"), lax.axis_size("expert") // NY
    total_tokens = tok * lax.axis_size(("expert", "seq", "dp"))
    hidden32 = hidden_in.astype(F32)
    normed = (
        hidden32
        * lax.rsqrt(jnp.mean(hidden32 * hidden32, axis=-1, keepdims=True) + 1e-06)
        * norm_gain
    ).astype(BF16)
    logits = jnp.dot(normed, router_weight, preferred_element_type=F32)
    picked = jnp.any(routes[:, :, None] == jnp.arange(n_experts, dtype=jnp.int32), axis=1)
    earlier = jnp.tril(jnp.ones((tok, tok), BF16), -1)
    place = jnp.dot(earlier, picked.astype(BF16), preferred_element_type=F32)
    affinity = jnp.where(picked, jax.nn.sigmoid(logits), 0.0)
    share = affinity / jnp.sum(affinity, axis=-1, keepdims=True)
    slots = jnp.arange(SLOTS, dtype=F32)
    where = picked[:, :, None] & (place[:, :, None] == slots)
    pick = where.reshape(tok, n_experts * SLOTS).astype(BF16)
    mix = jnp.where(where, share[:, :, None], 0.0).reshape(tok, n_experts * SLOTS)
    high = mix.astype(BF16)
    low = (mix - high.astype(F32)).astype(BF16)
    mix = jnp.concatenate([high, low], axis=0)
    outgoing = lax.dot_general(
        pick, normed, (((0,), (0,)), ((), ())), preferred_element_type=F32
    ).astype(BF16)

    student = (
        student_hidden.T.reshape(nz, NY, nx, 2, width // (2 * nx * NY * nz), tok)
        .transpose(2, 3, 1, 0, 4, 5)
        .reshape(nx, width // nx, tok)
    )
    return run(
        total_tokens,
        outgoing,
        mix,
        hidden_in,
        cached_layers,
        prediction,
        student,
        w_gate[0],
        w_up[0],
        w_down[0],
    )


def solution(mesh):
    tokens = P(("expert", "seq", "dp"), None)
    weights = P(("expert", "dp"), "seq", None)
    return jax.shard_map(
        body,
        mesh=mesh,
        in_specs=(
            tokens,
            P(),
            P(),
            tokens,
            weights,
            weights,
            weights,
            P(None, ("expert", "seq", "dp"), None),
            tokens,
            tokens,
        ),
        out_specs=(tokens, tokens),
        check_vma=False,
    )
```

```python
import functools
import math

import jax
import jax.numpy as jnp
from jax import lax
from jax.experimental import pallas as pl
from jax.experimental.pallas import tpu as pltpu
from jax.sharding import PartitionSpec as P

MESH = pl.DeviceIdType.MESH
F32, BF16 = jnp.float32, jnp.bfloat16
NY = 4


def wheel():
    e, x, c = lax.axis_index("expert"), lax.axis_index("seq"), lax.axis_index("dp")
    nx, nz = lax.axis_size("seq"), lax.axis_size("expert") // NY
    z, y = e // NY, lax.rem(e, NY)

    def to(z_, y_, x_, c_):
        return {"expert": z_ * NY + y_, "seq": x_, "dp": c_}

    def beside(q):
        return to(z, y, q // 2, lax.rem(q, 2))

    return {
        "c": (c, 2, lambda d: to(z, y, x, lax.rem(c + d, 2))),
        "w": (2 * x + c, 2 * nx, lambda d: beside(lax.rem(2 * x + c + d, 2 * nx))),
        "x": (x, nx, lambda d: to(z, y, lax.rem(x + d, nx), c)),
        "y": (y, NY, lambda d: to(z, lax.rem(y + d, NY), x, c)),
        "z": (z, nz, lambda d: to(lax.rem(z + d, nz), y, x, c)),
    }


def start_all(axis, source, target, send, recv):
    _, n, device = axis
    copies = []
    for d in range(1, n):
        copy = pltpu.make_async_remote_copy(
            src_ref=source(d),
            dst_ref=target(d),
            send_sem=send.at[d - 1],
            recv_sem=recv.at[d - 1],
            device_id=device(d),
            device_id_type=MESH,
        )
        copy.start()
        copies.append(copy)
    return copies


def wait_all(copies):
    for copy in copies:
        copy.wait()


def fold(row_list):
    w = row_list[0].shape[1] // 4
    return jnp.concatenate([r[:, i * w : (i + 1) * w] for r in row_list for i in range(4)], axis=0)


def unfold(block, row):
    return jnp.concatenate([block[4 * row + i : 4 * row + i + 1, :] for i in range(4)], axis=1)


def column_sums(values):
    return [jnp.sum(values, axis=0, keepdims=True), jnp.sum(values * values, axis=0, keepdims=True)]


SLOTS = 16
CHUNK = 512
TILE = 256


def normalise(hidden_ref, gain_ref, router_ref):
    hidden = hidden_ref[...].astype(F32)
    mean = jnp.mean(hidden * hidden, axis=-1, keepdims=True)
    normed = (hidden * lax.rsqrt(mean + 1e-6) * gain_ref[...]).astype(BF16)
    logits = lax.dot_general(
        normed, router_ref[...], (((1,), (1,)), ((), ())), preferred_element_type=F32
    )
    return normed, logits


def choose(routes_ref, logits, pick_ref, mix_ref):
    top, tok = routes_ref.shape
    experts = logits.shape[1]

    def index(shape, dim):
        return lax.broadcasted_iota(jnp.int32, shape, dim)

    def ones(flags):
        return jnp.where(flags, 1.0, 0.0)

    names = index((experts, tok), 0)
    chosen = jnp.zeros((experts, tok), F32)
    for k in range(top):
        chosen = chosen + ones(names == routes_ref[k : k + 1, :])
    square = (tok, tok)
    earlier = ones(index(square, 0) < index(square, 1)).astype(BF16)
    place = jnp.dot(chosen.astype(BF16), earlier, preferred_element_type=F32)
    code = jnp.where(chosen > 0.5, place, -1.0).astype(BF16)
    same = ones(index(square, 0) == index(square, 1)).astype(BF16)
    code_of = lax.dot_general(same, code, (((1,), (1,)), ((), ())), preferred_element_type=F32)
    tall, wide = (experts * SLOTS, experts), (experts, experts * SLOTS)
    spread_rows = ones(index(tall, 0) // SLOTS == index(tall, 1)).astype(BF16)
    spread = ones(index(wide, 1) // SLOTS == index(wide, 0)).astype(BF16)
    rows = jnp.dot(spread_rows, code, preferred_element_type=F32)
    slots = lax.rem(index(rows.shape, 0), SLOTS).astype(F32)
    pick_ref[...] = ones(rows == slots).astype(BF16)
    affinity = jnp.where(code_of > -0.5, jax.nn.sigmoid(logits), 0.0)
    share = affinity / jnp.sum(affinity, axis=-1, keepdims=True)
    high = share.astype(BF16)
    low = (share - high.astype(F32)).astype(BF16)
    columns = jnp.dot(code_of.astype(BF16), spread, preferred_element_type=F32)
    match = columns == lax.rem(index(columns.shape, 1), SLOTS).astype(F32)
    for i, part in enumerate((high, low)):
        shares = jnp.dot(part, spread, preferred_element_type=F32)
        mix_ref[i * tok : (i + 1) * tok, :] = jnp.where(match, shares, 0.0).astype(BF16)


def kernel(
    total_tokens,
    gain_ref,
    router_ref,
    routes_ref,
    hidden_ref,
    cached_ref,
    prediction_ref,
    student_ref,
    wg_ref,
    wu_ref,
    wd_ref,
    targets_ref,
    grad_ref,
    wg,
    wu,
    wd,
    pick_ref,
    mix_ref,
    blocks,
    picks,
    arrived,
    gated,
    raised,
    act,
    out,
    back,
    layer_out,
    cached_own,
    cached_w,
    cached_y,
    cached_z,
    stat_own,
    stat_w,
    stat_y,
    stat_z,
    students,
    residuals,
    from_c,
    from_y,
    from_z,
    sem_own,
    sem_w,
    sem_ring,
    sem_pick,
    sem_rows,
    sem_back,
    sem_st,
    sem_s,
    sem_x,
    sem_c,
    sem_y,
    sem_z,
):
    axes = wheel()
    tok, width = hidden_ref.shape
    window = prediction_ref.shape[1]
    e, x, c = lax.axis_index("expert"), lax.axis_index("seq"), lax.axis_index("dp")
    nx = axes["x"][1]
    n = 2 * lax.axis_size("expert")
    me = 2 * e + c
    half = width // 2
    z, nz, z_device = axes["z"]
    y, ny, _ = axes["y"]

    def peer(d):
        p = lax.rem(me + d, n)
        return p, {"expert": p // 2, "seq": x, "dp": lax.rem(p, 2)}

    barrier = pltpu.get_barrier_semaphore()

    def greet(d, _):
        pl.semaphore_signal(barrier, inc=1, device_id=peer(d)[1], device_id_type=MESH)
        return _

    lax.fori_loop(1, n, greet, 0)
    for d in range(1, 2 * nx):
        pl.semaphore_signal(barrier, inc=1, device_id=axes["w"][2](d), device_id_type=MESH)
    pl.semaphore_wait(barrier, n - 1 + 2 * nx - 1)

    right, left = axes["x"][2](1), axes["x"][2](nx - 1)
    before, after = lax.rem(x + nx - 1, nx), lax.rem(x + 1, nx)

    def weight_piece(number, shard, whole, cols):
        rows = shard.shape[0]
        cut = rows // 2

        def at(origin, part):
            return pl.ds(pl.multiple_of(origin * rows + part * cut, 16), cut)

        def copy(i, source, origin, part, device):
            return pltpu.make_async_remote_copy(
                src_ref=source,
                dst_ref=whole.at[at(origin, part), cols],
                send_sem=sem_w.at[number, 0, i],
                recv_sem=sem_w.at[number, 1, i],
                device_id=device,
                device_id_type=MESH,
            )

        def own(part):
            return shard.at[pl.ds(part * cut, cut), cols]

        def passed(origin, part):
            return whole.at[at(origin, part), cols]

        return [
            copy(0, own(0), x, 0, right),
            copy(1, own(1), x, 1, right),
            copy(2, own(1), x, 1, left),
            copy(3, own(0), x, 0, left),
            copy(4, passed(before, 0), before, 0, right),
            copy(5, passed(after, 1), after, 1, left),
        ]

    def begin(piece):
        for i in (0, 2, 1, 3):
            piece[i].start()

    def pass_on(piece):
        piece[0].wait_recv()
        piece[4].start()
        piece[2].wait_recv()
        piece[5].start()

    every = slice(0, wg.shape[1])
    gate_piece = weight_piece(0, wg_ref, wg, every)
    up_piece = weight_piece(1, wu_ref, wu, every)
    chunks = width // CHUNK
    down_pieces = [
        weight_piece(2 + i, wd_ref, wd, slice(i * CHUNK, (i + 1) * CHUNK)) for i in range(chunks)
    ]
    begin(gate_piece)
    blocks[z], logits = normalise(hidden_ref, gain_ref, router_ref)
    choose(routes_ref, logits, pick_ref, mix_ref)

    def block(p):
        return pl.ds(pl.multiple_of(p * SLOTS, SLOTS), SLOTS)

    def scatter(source, target, cols, send, recv):
        def go(d, _):
            p, device = peer(d)
            pltpu.make_async_remote_copy(
                src_ref=source.at[block(p), cols],
                dst_ref=target.at[block(me), cols],
                send_sem=send,
                recv_sem=recv,
                device_id=device,
                device_id_type=MESH,
            ).start()
            return _

        lax.fori_loop(1, n, go, 0)
        target[block(me), cols] = source[block(me), cols]

    def wait_rows(ref, count, cols, sem):
        rows = ref.at[pl.ds(0, count * SLOTS), cols]
        pltpu.make_async_copy(rows, rows, sem).wait()

    group = 2 * ny * SLOTS
    half_block = tok // 2
    last = nz - 2

    def ring(way, m):
        s, part = m // 2, (m + way) % 2
        b = lax.rem(z + (nz - s if way == 0 else s), nz)
        rows = blocks.at[b, pl.ds(part * half_block, half_block)]
        return pltpu.make_async_remote_copy(
            src_ref=rows,
            dst_ref=rows,
            send_sem=sem_ring.at[0, way, m],
            recv_sem=sem_ring.at[1, way, m],
            device_id=z_device(1 if way == 0 else nz - 1),
            device_id_type=MESH,
        )

    rings = [[ring(way, m) for m in range(last + 1)] for way in range(2)]

    def group_rows(b):
        return pl.ds(pl.multiple_of(b * group, group), group)

    def start_ring(m):
        for way in range(2):
            rings[way][m].start()

    def next_ring(m):
        for way in range(2):
            rings[way][m].wait_recv()
            if m + 2 <= last:
                rings[way][m + 2].start()

    def select(b):
        for j in range(chunks):
            cols = slice(j * CHUNK, (j + 1) * CHUNK)
            out[group_rows(b), cols] = jnp.dot(
                picks[b], blocks[b, :, cols], preferred_element_type=F32
            ).astype(BF16)
        p = (b * ny + y) * 2 + c

        def go(d, _):
            q = lax.rem(2 * y + c + d, 2 * ny)
            pltpu.make_async_remote_copy(
                src_ref=out.at[block(b * 2 * ny + q)],
                dst_ref=arrived.at[block(p)],
                send_sem=sem_rows.at[0],
                recv_sem=sem_rows.at[1],
                device_id={"expert": z * ny + q // 2, "seq": x, "dp": lax.rem(q, 2)},
                device_id_type=MESH,
            ).start()
            return _

        lax.fori_loop(1, 2 * ny, go, 0)
        arrived[block(p), :] = out[block(b * 2 * ny + 2 * y + c), :]

    picks_out = start_all(
        axes["z"],
        lambda d: pick_ref.at[group_rows(lax.rem(z + d, nz))],
        lambda d: picks.at[z],
        sem_pick.at[0],
        sem_pick.at[1],
    )
    start_ring(0)
    start_ring(1)
    picks[z] = pick_ref[group_rows(z), :]
    mine = []
    for i, (shard, whole) in enumerate(((wg_ref, wg), (wu_ref, wu), (wd_ref, wd))):
        rows = shard.shape[0]
        copy = pltpu.make_async_copy(
            shard, whole.at[pl.ds(pl.multiple_of(x * rows, 16), rows)], sem_own.at[i]
        )
        copy.start()
        mine.append(copy)
    students_out = start_all(
        axes["x"],
        lambda d: student_ref.at[lax.rem(x + d, nx)],
        lambda d: students.at[d],
        sem_st.at[0],
        sem_st.at[1],
    )
    students[0] = student_ref[x]

    def add_over_devices(number, own, slots):
        for i, name in enumerate("wyz"):
            copies = start_all(
                axes[name],
                lambda d: own.at[i],
                lambda d: slots[i].at[d - 1],
                sem_s.at[number, i, 0],
                sem_s.at[number, i, 1],
            )
            wait_all(copies)
            total = own[i]
            for d in range(1, axes[name][1]):
                total = total + slots[i][d - 1]
            own[i + 1] = total

    stats = []
    for layer in range(3):
        stats += column_sums(cached_ref[layer].astype(F32))
    cached_own[0] = fold(stats)

    for copy in picks_out:
        copy.wait_recv()
    select(z)
    for m in range(2):
        next_ring(m)
    select(lax.rem(z + nz - 1, nz))
    select(lax.rem(z + 1, nz))
    for m in range(2, 4):
        next_ring(m)
    select(lax.rem(z + nz - 2, nz))
    select(lax.rem(z + 2, nz))
    pass_on(gate_piece)
    for m in range(4, 6):
        next_ring(m)
    select(lax.rem(z + nz - 3, nz))
    select(lax.rem(z + 3, nz))
    gate_piece[1].wait_recv()
    gate_piece[3].wait_recv()
    begin(up_piece)
    next_ring(6)
    select(lax.rem(z + nz // 2, nz))
    add_over_devices(0, cached_own, (cached_w, cached_y, cached_z))
    for copy in mine:
        copy.wait()
    gate_piece[4].wait_recv()
    gate_piece[5].wait_recv()
    everything = slice(0, width)
    wait_rows(arrived, n - nz, everything, sem_rows.at[1])

    def gate_tile(i, _):
        at = pl.ds(pl.multiple_of(i * TILE, TILE), TILE)
        gate = jnp.dot(arrived[at, :], wg[...], preferred_element_type=F32)
        gated[at, :] = gate * jax.nn.sigmoid(gate)
        return _

    shard = wu_ref.shape[0]

    def up_part(at, origin):
        rows = pl.ds(pl.multiple_of(origin * shard, shard), shard)
        return jnp.dot(arrived[at, rows], wu[rows, :], preferred_element_type=F32)

    def up_tile(i, _):
        at = pl.ds(pl.multiple_of(i * TILE, TILE), TILE)
        raised[at, :] = up_part(at, x) + up_part(at, before) + up_part(at, after)
        return _

    def act_tile(i, _):
        at = pl.ds(pl.multiple_of(i * TILE, TILE), TILE)
        up = raised[at, :] + up_part(at, lax.rem(x + 2, nx))
        act[at, :] = (gated[at, :] * up).astype(BF16)
        return _

    tiles = arrived.shape[0] // TILE
    lax.fori_loop(0, tiles // 2, gate_tile, 0)
    pass_on(up_piece)
    lax.fori_loop(tiles // 2, tiles, gate_tile, 0)
    up_piece[1].wait_recv()
    up_piece[3].wait_recv()
    begin(down_pieces[0])
    lax.fori_loop(0, tiles, up_tile, 0)
    up_piece[4].wait_recv()
    up_piece[5].wait_recv()
    begin(down_pieces[1])
    lax.fori_loop(0, tiles, act_tile, 0)
    wait_rows(out, n - nz, everything, sem_rows.at[0])
    pass_on(down_pieces[0])

    def send_back(j):
        cols = slice(j * CHUNK, (j + 1) * CHUNK)
        scatter(out, back, cols, sem_back.at[0, j], sem_back.at[1, j])

    for j in range(chunks):
        if j + 2 < chunks:
            begin(down_pieces[j + 2])
        for i in (1, 3, 4, 5):
            down_pieces[j][i].wait_recv()
        cols = slice(j * CHUNK, (j + 1) * CHUNK)

        def project(i, _):
            at = pl.ds(pl.multiple_of(i * TILE, TILE), TILE)
            out[at, cols] = jnp.dot(act[at, :], wd[:, cols], preferred_element_type=F32).astype(BF16)
            return _

        lax.fori_loop(0, tiles, project, 0)
        if j < chunks // 2:
            send_back(j)
        if j + 1 < chunks:
            pass_on(down_pieces[j + 1])

    for j in range(chunks // 2):
        wait_rows(out, n - 1, slice(j * CHUNK, (j + 1) * CHUNK), sem_back.at[0, j])
    for j in range(chunks // 2, chunks):
        send_back(j)
    scale = 1.0 / math.sqrt(total_tokens)
    tail_cut = 4

    def combine(h):
        for j in range(h * chunks // 2, (h + 1) * chunks // 2):
            cols = slice(j * CHUNK, (j + 1) * CHUNK)
            wait_rows(back, n - 1, cols, sem_back.at[1, j])
            both = jnp.dot(mix_ref[...], back[:, cols], preferred_element_type=F32)
            layer_out[:, cols] = hidden_ref[:, cols].astype(F32) + (both[:tok] + both[tok:])
        stat_own[h, 0] = fold(column_sums(layer_out[:, h * half : (h + 1) * half]))

    def add_statistics(h):
        slots = [s.at[h] for s in (stat_w, stat_y, stat_z)]
        add_over_devices(1 + h, stat_own.at[h], slots)

    def write_targets(h):
        last = stat_own[h, 3]
        earlier = cached_own[3]
        w = half // tail_cut
        for j in range(h * chunks // 2, (h + 1) * chunks // 2):
            cols = slice(j * CHUNK, (j + 1) * CHUNK)
            summed = jnp.zeros((tok, CHUNK), F32)
            for layer in range(4):
                if layer < 3:
                    sums = earlier[8 * layer + j : 8 * layer + j + 1, :]
                    squares = earlier[8 * layer + 4 + j : 8 * layer + 5 + j, :]
                    values = cached_ref[layer, :, cols].astype(F32)
                else:
                    k = (j - h * chunks // 2) * (CHUNK // w)
                    sums = jnp.concatenate([last[k : k + 1], last[k + 1 : k + 2]], axis=1)
                    squares = jnp.concatenate([last[4 + k : 5 + k], last[5 + k : 6 + k]], axis=1)
                    values = layer_out[:, cols]
                mean = sums / total_tokens
                variance = squares / total_tokens - mean * mean
                summed = summed + (values - mean) * lax.rsqrt(variance + 1e-5)
            targets = (summed * 0.25).astype(BF16)
            targets_ref[:, cols] = targets
            if (j + 1) * CHUNK <= window:
                residuals[0, :, cols] = (
                    (prediction_ref[:, cols].astype(F32) - targets.astype(F32)) * scale
                ).astype(BF16)

    combine(0)
    add_statistics(0)
    write_targets(0)
    copies = start_all(
        axes["x"],
        lambda d: residuals.at[0],
        lambda d: residuals.at[d],
        sem_x.at[0],
        sem_x.at[1],
    )
    wait_all(students_out)
    rows = students.shape[1]
    partial = raised.at[pl.ds(0, rows), pl.ds(0, window)]
    halved = rows // 2
    for d in range(nx):
        if d:
            copies[d - 1].wait_recv()

        def add(i, _):
            at = pl.ds(pl.multiple_of(i * 128, 128), 128)
            product = jnp.dot(students[d, at, :], residuals[d], preferred_element_type=F32)
            partial[at, :] = product if d == 0 else partial[at, :] + product
            return _

        lax.fori_loop(0, rows // 128, add, 0)
    for copy in copies:
        copy.wait_send()
    other = pl.ds(pl.multiple_of((1 - c) * halved, halved), halved)
    kept = pl.ds(pl.multiple_of(c * halved, halved), halved)
    wait_all(
        start_all(
            axes["c"],
            lambda d: partial.at[other],
            lambda d: from_c,
            sem_c.at[0],
            sem_c.at[1],
        )
    )
    from_c[...] = from_c[...] + partial[kept, :]
    part = halved // ny

    def y_rows(d):
        return pl.ds(pl.multiple_of(lax.rem(y + d, ny) * part, part), part)

    copies = start_all(
        axes["y"],
        lambda d: from_c.at[y_rows(d)],
        lambda d: from_y.at[d],
        sem_y.at[0],
        sem_y.at[1],
    )
    combine(1)
    add_statistics(1)
    wait_all(copies)
    total = from_c[y_rows(0), :]
    for d in range(1, ny):
        total = total + from_y[d]
    from_y[0] = total
    least = part // nz

    def z_rows(d):
        return pl.ds(pl.multiple_of(lax.rem(z + d, nz) * least, least), least)

    copies = start_all(
        axes["z"],
        lambda d: from_y.at[0, z_rows(d)],
        lambda d: from_z.at[d],
        sem_z.at[0],
        sem_z.at[1],
    )
    write_targets(1)
    wait_all(copies)
    total = from_y[0, z_rows(0), :]
    for d in range(1, nz):
        total = total + from_z[d]
    grad_ref[...] = total

    for piece in (gate_piece, up_piece, *down_pieces):
        for copy in piece:
            copy.wait_send()
    for copy in (*picks_out, *rings[0], *rings[1]):
        copy.wait_send()
    for j in range(chunks // 2, chunks):
        wait_rows(out, n - 1, slice(j * CHUNK, (j + 1) * CHUNK), sem_back.at[0, j])


def run(total_tokens, gain, router, routes, hidden_in, cached, prediction, student, wg, wu, wd):
    tok, width = hidden_in.shape
    window = prediction.shape[1]
    nx, ny, nz = lax.axis_size("seq"), NY, lax.axis_size("expert") // NY
    rows = width // nx
    hidden_units = wg.shape[1]
    arrived = router.shape[0] * SLOTS
    chunks = width // CHUNK
    vmem = pl.BlockSpec(memory_space=pltpu.VMEM)
    hbm = pl.BlockSpec(memory_space=pl.ANY)
    dma = pltpu.SemaphoreType.DMA
    early, late = (24, width // 4), (8, width // 8)
    return pl.pallas_call(
        functools.partial(kernel, total_tokens),
        out_shape=(
            jax.ShapeDtypeStruct((tok, width), BF16),
            jax.ShapeDtypeStruct((rows // (2 * ny * nz), window), F32),
        ),
        in_specs=[vmem] * 7 + [hbm] * 3,
        out_specs=(vmem, vmem),
        scratch_shapes=[
            pltpu.VMEM((width, hidden_units), BF16),
            pltpu.VMEM((width, hidden_units), BF16),
            pltpu.VMEM((hidden_units, width), BF16),
            pltpu.VMEM((arrived, tok), BF16),
            pltpu.VMEM((2 * tok, arrived), BF16),
            pltpu.VMEM((nz, tok, width), BF16),
            pltpu.VMEM((nz, arrived // nz, tok), BF16),
            pltpu.VMEM((arrived, width), BF16),
            pltpu.VMEM((arrived, hidden_units), F32),
            pltpu.VMEM((arrived, hidden_units), F32),
            pltpu.VMEM((arrived, hidden_units), BF16),
            pltpu.VMEM((arrived, width), BF16),
            pltpu.VMEM((arrived, width), BF16),
            pltpu.VMEM((tok, width), F32),
            pltpu.VMEM((4, *early), F32),
            pltpu.VMEM((2 * nx - 1, *early), F32),
            pltpu.VMEM((ny - 1, *early), F32),
            pltpu.VMEM((nz - 1, *early), F32),
            pltpu.VMEM((2, 4, *late), F32),
            pltpu.VMEM((2, 2 * nx - 1, *late), F32),
            pltpu.VMEM((2, ny - 1, *late), F32),
            pltpu.VMEM((2, nz - 1, *late), F32),
            pltpu.VMEM((nx, rows, tok), BF16),
            pltpu.VMEM((nx, tok, window), BF16),
            pltpu.VMEM((rows // 2, window), F32),
            pltpu.VMEM((ny, rows // (2 * ny), window), F32),
            pltpu.VMEM((nz, rows // (2 * ny * nz), window), F32),
            dma((3,)),
            dma((2 + chunks, 2, 6)),
            dma((2, 2, nz - 1)),
            dma((2, nz - 1)),
            dma((2,)),
            dma((2, chunks)),
            dma((2, nx - 1)),
            dma((3, 3, 2, 7)),
            dma((2, nx - 1)),
            dma((2, 1)),
            dma((2, ny - 1)),
            dma((2, nz - 1)),
        ],
        compiler_params=pltpu.CompilerParams(
            collective_id=1, has_side_effects=True, vmem_limit_bytes=60 * 2**20
        ),
    )(gain, router, routes, hidden_in, cached, prediction, student, wg, wu, wd)


def body(
    hidden_in,
    norm_gain,
    router_weight,
    routes,
    w_gate,
    w_up,
    w_down,
    cached_layers,
    student_hidden,
    prediction,
):
    tok, width = hidden_in.shape
    nx, nz = lax.axis_size("seq"), lax.axis_size("expert") // NY
    total_tokens = tok * lax.axis_size(("expert", "seq", "dp"))
    student = (
        student_hidden.T.reshape(nz, NY, nx, 2, width // (2 * nx * NY * nz), tok)
        .transpose(2, 3, 1, 0, 4, 5)
        .reshape(nx, width // nx, tok)
    )
    return run(
        total_tokens,
        norm_gain[None],
        router_weight.T,
        routes.T,
        hidden_in,
        cached_layers,
        prediction,
        student,
        w_gate[0],
        w_up[0],
        w_down[0],
    )


def solution(mesh):
    tokens = P(("expert", "seq", "dp"), None)
    weights = P(("expert", "dp"), "seq", None)
    return jax.shard_map(
        body,
        mesh=mesh,
        in_specs=(
            tokens,
            P(),
            P(),
            tokens,
            weights,
            weights,
            weights,
            P(None, ("expert", "seq", "dp"), None),
            tokens,
            tokens,
        ),
        out_specs=(tokens, tokens),
        check_vma=False,
    )
```

```python
import functools
import math

import jax
import jax.numpy as jnp
from jax import lax
from jax.experimental import pallas as pl
from jax.experimental.pallas import tpu as pltpu
from jax.sharding import PartitionSpec as P

MESH = pl.DeviceIdType.MESH
F32, BF16 = jnp.float32, jnp.bfloat16
NY = 4


def wheel():
    e, x, c = lax.axis_index("expert"), lax.axis_index("seq"), lax.axis_index("dp")
    nx, nz = lax.axis_size("seq"), lax.axis_size("expert") // NY
    z, y = e // NY, lax.rem(e, NY)

    def to(z_, y_, x_, c_):
        return {"expert": z_ * NY + y_, "seq": x_, "dp": c_}

    def beside(q):
        return to(z, y, q // 2, lax.rem(q, 2))

    return {
        "c": (c, 2, lambda d: to(z, y, x, lax.rem(c + d, 2))),
        "w": (2 * x + c, 2 * nx, lambda d: beside(lax.rem(2 * x + c + d, 2 * nx))),
        "x": (x, nx, lambda d: to(z, y, lax.rem(x + d, nx), c)),
        "y": (y, NY, lambda d: to(z, lax.rem(y + d, NY), x, c)),
        "z": (z, nz, lambda d: to(lax.rem(z + d, nz), y, x, c)),
    }


def start_all(axis, source, target, send, recv):
    _, n, device = axis
    copies = []
    for d in range(1, n):
        copy = pltpu.make_async_remote_copy(
            src_ref=source(d),
            dst_ref=target(d),
            send_sem=send.at[d - 1],
            recv_sem=recv.at[d - 1],
            device_id=device(d),
            device_id_type=MESH,
        )
        copy.start()
        copies.append(copy)
    return copies


def wait_all(copies):
    for copy in copies:
        copy.wait()


def fold(row_list):
    w = row_list[0].shape[1] // 4
    return jnp.concatenate([r[:, i * w : (i + 1) * w] for r in row_list for i in range(4)], axis=0)


def unfold(block, row):
    return jnp.concatenate([block[4 * row + i : 4 * row + i + 1, :] for i in range(4)], axis=1)


def column_sums(values):
    return [jnp.sum(values, axis=0, keepdims=True), jnp.sum(values * values, axis=0, keepdims=True)]


SLOTS = 16
CHUNK = 512
STRIDE = 27
TILE = 256


def normalise(hidden_ref, gain_ref, router_ref):
    hidden = hidden_ref[...].astype(F32)
    mean = jnp.mean(hidden * hidden, axis=-1, keepdims=True)
    normed = (hidden * lax.rsqrt(mean + 1e-6) * gain_ref[...]).astype(BF16)
    logits = lax.dot_general(
        normed, router_ref[...], (((1,), (1,)), ((), ())), preferred_element_type=F32
    )
    return normed, logits


def choose(routes_ref, logits, pick_ref, mix_ref):
    top, tok = routes_ref.shape
    experts = logits.shape[1]

    def index(shape, dim):
        return lax.broadcasted_iota(jnp.int32, shape, dim)

    def ones(flags):
        return jnp.where(flags, 1.0, 0.0)

    names = index((experts, tok), 0)
    chosen = jnp.zeros((experts, tok), F32)
    for k in range(top):
        chosen = chosen + ones(names == routes_ref[k : k + 1, :])
    square = (tok, tok)
    earlier = ones(index(square, 0) < index(square, 1)).astype(BF16)
    place = jnp.dot(chosen.astype(BF16), earlier, preferred_element_type=F32)
    code = jnp.where(chosen > 0.5, place, -1.0).astype(BF16)
    same = ones(index(square, 0) == index(square, 1)).astype(BF16)
    code_of = lax.dot_general(same, code, (((1,), (1,)), ((), ())), preferred_element_type=F32)
    tall, wide = (experts * SLOTS, experts), (experts, experts * SLOTS)
    spread_rows = ones(index(tall, 0) // SLOTS == index(tall, 1)).astype(BF16)
    spread = ones(index(wide, 1) // SLOTS == index(wide, 0)).astype(BF16)
    rows = jnp.dot(spread_rows, code, preferred_element_type=F32)
    slots = lax.rem(index(rows.shape, 0), SLOTS).astype(F32)
    pick_ref[...] = ones(rows == slots).astype(BF16)
    affinity = jnp.where(code_of > -0.5, jax.nn.sigmoid(logits), 0.0)
    share = affinity / jnp.sum(affinity, axis=-1, keepdims=True)
    high = share.astype(BF16)
    low = (share - high.astype(F32)).astype(BF16)
    columns = jnp.dot(code_of.astype(BF16), spread, preferred_element_type=F32)
    match = columns == lax.rem(index(columns.shape, 1), SLOTS).astype(F32)
    for i, part in enumerate((high, low)):
        shares = jnp.dot(part, spread, preferred_element_type=F32)
        mix_ref[i * tok : (i + 1) * tok, :] = jnp.where(match, shares, 0.0).astype(BF16)


def kernel(
    total_tokens,
    gain_ref,
    router_ref,
    routes_ref,
    hidden_ref,
    cached_ref,
    prediction_ref,
    student_ref,
    wg_ref,
    wu_ref,
    wd_ref,
    targets_ref,
    grad_ref,
    wg,
    wu,
    wd,
    pick_ref,
    mix_ref,
    blocks,
    picks,
    arrived,
    gated,
    raised,
    act,
    out,
    back,
    layer_out,
    cached_own,
    cached_w,
    cached_y,
    cached_z,
    stat_own,
    stat_w,
    stat_y,
    stat_z,
    students,
    residuals,
    from_c,
    from_y,
    from_z,
    sem_own,
    sem_w,
    sem_ring,
    sem_pick,
    sem_rows,
    sem_back,
    sem_st,
    sem_s,
    sem_x,
    sem_c,
    sem_y,
    sem_z,
):
    axes = wheel()
    tok, width = hidden_ref.shape
    window = prediction_ref.shape[1]
    e, x, c = lax.axis_index("expert"), lax.axis_index("seq"), lax.axis_index("dp")
    nx = axes["x"][1]
    n = 2 * lax.axis_size("expert")
    me = 2 * e + c
    half = width // 2
    z, nz, z_device = axes["z"]
    y, ny, _ = axes["y"]

    def peer(d):
        p = lax.rem(me + d, n)
        return p, {"expert": p // 2, "seq": x, "dp": lax.rem(p, 2)}

    barrier = pltpu.get_barrier_semaphore()

    def greet(d, _):
        pl.semaphore_signal(barrier, inc=1, device_id=peer(d)[1], device_id_type=MESH)
        return _

    lax.fori_loop(1, n, greet, 0)
    for d in range(1, 2 * nx):
        pl.semaphore_signal(barrier, inc=1, device_id=axes["w"][2](d), device_id_type=MESH)
    pl.semaphore_wait(barrier, n - 1 + 2 * nx - 1)

    right, left = axes["x"][2](1), axes["x"][2](nx - 1)
    before, after = lax.rem(x + nx - 1, nx), lax.rem(x + 1, nx)

    def weight_piece(number, shard, whole, cols):
        rows = shard.shape[0]
        cut = rows // 2

        def at(origin, part):
            return pl.ds(pl.multiple_of(origin * rows + part * cut, 16), cut)

        def copy(i, source, origin, part, device):
            return pltpu.make_async_remote_copy(
                src_ref=source,
                dst_ref=whole.at[at(origin, part), cols],
                send_sem=sem_w.at[number, 0, i],
                recv_sem=sem_w.at[number, 1, i],
                device_id=device,
                device_id_type=MESH,
            )

        def own(part):
            return shard.at[pl.ds(part * cut, cut), cols]

        def passed(origin, part):
            return whole.at[at(origin, part), cols]

        return [
            copy(0, own(0), x, 0, right),
            copy(1, own(1), x, 1, right),
            copy(2, own(1), x, 1, left),
            copy(3, own(0), x, 0, left),
            copy(4, passed(before, 0), before, 0, right),
            copy(5, passed(after, 1), after, 1, left),
        ]

    def begin(piece):
        for i in (0, 2, 1, 3):
            piece[i].start()

    def pass_on(piece):
        piece[0].wait_recv()
        piece[4].start()
        piece[2].wait_recv()
        piece[5].start()

    every = slice(0, wg.shape[1])
    gate_piece = weight_piece(0, wg_ref, wg, every)
    up_piece = weight_piece(1, wu_ref, wu, every)
    chunks = width // CHUNK
    down_pieces = [
        weight_piece(2 + i, wd_ref, wd, slice(i * CHUNK, (i + 1) * CHUNK)) for i in range(chunks)
    ]
    begin(gate_piece)
    blocks[z], logits = normalise(hidden_ref, gain_ref, router_ref)
    choose(routes_ref, logits, pick_ref, mix_ref)

    def block(p):
        return pl.ds(pl.multiple_of(p * SLOTS, SLOTS), SLOTS)

    def scatter(source, target, cols, send, recv, first, end):
        def go(i, _):
            p, device = peer(lax.rem(i * STRIDE, n))
            pltpu.make_async_remote_copy(
                src_ref=source.at[block(p), cols],
                dst_ref=target.at[block(me), cols],
                send_sem=send,
                recv_sem=recv,
                device_id=device,
                device_id_type=MESH,
            ).start()
            return _

        lax.fori_loop(first, end, go, 0)
        if first == 1:
            target[block(me), cols] = source[block(me), cols]

    def wait_rows(ref, count, cols, sem):
        rows = ref.at[pl.ds(0, count * SLOTS), cols]
        pltpu.make_async_copy(rows, rows, sem).wait()

    group = 2 * ny * SLOTS
    half_block = tok // 2
    last = nz - 2

    def ring(way, m):
        s, part = m // 2, (m + way) % 2
        b = lax.rem(z + (nz - s if way == 0 else s), nz)
        rows = blocks.at[b, pl.ds(part * half_block, half_block)]
        return pltpu.make_async_remote_copy(
            src_ref=rows,
            dst_ref=rows,
            send_sem=sem_ring.at[0, way, m],
            recv_sem=sem_ring.at[1, way, m],
            device_id=z_device(1 if way == 0 else nz - 1),
            device_id_type=MESH,
        )

    rings = [[ring(way, m) for m in range(last + 1)] for way in range(2)]

    def group_rows(b):
        return pl.ds(pl.multiple_of(b * group, group), group)

    def start_ring(m):
        for way in range(2):
            rings[way][m].start()

    def next_ring(m):
        for way in range(2):
            rings[way][m].wait_recv()
            if m + 2 <= last:
                rings[way][m + 2].start()

    def select(b):
        for j in range(chunks):
            cols = slice(j * CHUNK, (j + 1) * CHUNK)
            out[group_rows(b), cols] = jnp.dot(
                picks[b], blocks[b, :, cols], preferred_element_type=F32
            ).astype(BF16)
        p = (b * ny + y) * 2 + c

        def go(d, _):
            q = lax.rem(2 * y + c + d, 2 * ny)
            pltpu.make_async_remote_copy(
                src_ref=out.at[block(b * 2 * ny + q)],
                dst_ref=arrived.at[block(p)],
                send_sem=sem_rows.at[0],
                recv_sem=sem_rows.at[1],
                device_id={"expert": z * ny + q // 2, "seq": x, "dp": lax.rem(q, 2)},
                device_id_type=MESH,
            ).start()
            return _

        lax.fori_loop(1, 2 * ny, go, 0)
        arrived[block(p), :] = out[block(b * 2 * ny + 2 * y + c), :]

    picks_out = start_all(
        axes["z"],
        lambda d: pick_ref.at[group_rows(lax.rem(z + d, nz))],
        lambda d: picks.at[z],
        sem_pick.at[0],
        sem_pick.at[1],
    )
    start_ring(0)
    start_ring(1)
    picks[z] = pick_ref[group_rows(z), :]
    mine = []
    for i, (shard, whole) in enumerate(((wg_ref, wg), (wu_ref, wu), (wd_ref, wd))):
        rows = shard.shape[0]
        copy = pltpu.make_async_copy(
            shard, whole.at[pl.ds(pl.multiple_of(x * rows, 16), rows)], sem_own.at[i]
        )
        copy.start()
        mine.append(copy)
    students_out = start_all(
        axes["x"],
        lambda d: student_ref.at[lax.rem(x + d, nx)],
        lambda d: students.at[d],
        sem_st.at[0],
        sem_st.at[1],
    )
    students[0] = student_ref[x]

    def add_over_devices(number, own, slots):
        for i, name in enumerate("wyz"):
            copies = start_all(
                axes[name],
                lambda d: own.at[i],
                lambda d: slots[i].at[d - 1],
                sem_s.at[number, i, 0],
                sem_s.at[number, i, 1],
            )
            yield
            wait_all(copies)
            total = own[i]
            for d in range(1, axes[name][1]):
                total = total + slots[i][d - 1]
            own[i + 1] = total

    stats = []
    for layer in range(3):
        stats += column_sums(cached_ref[layer].astype(F32))
    cached_own[0] = fold(stats)

    for copy in picks_out:
        copy.wait_recv()
    select(z)
    next_ring(0)
    next_ring(1)
    select(lax.rem(z + nz - 1, nz))
    select(lax.rem(z + 1, nz))
    pass_on(gate_piece)
    next_ring(2)
    next_ring(3)
    select(lax.rem(z + nz - 2, nz))
    select(lax.rem(z + 2, nz))
    next_ring(4)
    next_ring(5)
    gate_piece[1].wait_recv()
    gate_piece[3].wait_recv()
    begin(up_piece)
    select(lax.rem(z + nz - 3, nz))
    select(lax.rem(z + 3, nz))
    next_ring(6)
    select(lax.rem(z + nz // 2, nz))
    cached_sums = add_over_devices(0, cached_own, (cached_w, cached_y, cached_z))
    next(cached_sums, None)
    for copy in mine:
        copy.wait()
    gate_piece[4].wait_recv()
    gate_piece[5].wait_recv()
    pass_on(up_piece)
    everything = slice(0, width)
    wait_rows(arrived, n - nz, everything, sem_rows.at[1])

    def gate_tile(i, _):
        at = pl.ds(pl.multiple_of(i * TILE, TILE), TILE)
        gate = jnp.dot(arrived[at, :], wg[...], preferred_element_type=F32)
        gated[at, :] = gate * jax.nn.sigmoid(gate)
        return _

    shard = wu_ref.shape[0]

    def up_part(at, origin):
        rows = pl.ds(pl.multiple_of(origin * shard, shard), shard)
        return jnp.dot(arrived[at, rows], wu[rows, :], preferred_element_type=F32)

    def up_tile(i, _):
        at = pl.ds(pl.multiple_of(i * TILE, TILE), TILE)
        raised[at, :] = up_part(at, x) + up_part(at, before) + up_part(at, after)
        return _

    def act_tile(i, _):
        at = pl.ds(pl.multiple_of(i * TILE, TILE), TILE)
        up = raised[at, :] + up_part(at, lax.rem(x + 2, nx))
        act[at, :] = (gated[at, :] * up).astype(BF16)
        return _

    tiles = arrived.shape[0] // TILE
    next(cached_sums, None)
    lax.fori_loop(0, tiles, gate_tile, 0)
    next(cached_sums, None)
    up_piece[1].wait_recv()
    up_piece[3].wait_recv()
    begin(down_pieces[0])
    lax.fori_loop(0, tiles, up_tile, 0)
    next(cached_sums, None)
    up_piece[4].wait_recv()
    up_piece[5].wait_recv()
    begin(down_pieces[1])
    lax.fori_loop(0, tiles, act_tile, 0)
    wait_rows(out, n - nz, everything, sem_rows.at[0])

    def columns_of(j):
        return slice(j * CHUNK, (j + 1) * CHUNK)

    def send_back(j, first, end):
        scatter(out, back, columns_of(j), sem_back.at[0, j], sem_back.at[1, j], first, end)

    def project(j):
        for i in (1, 3, 4, 5):
            down_pieces[j][i].wait_recv()
        cols = columns_of(j)

        def project_tile(i, _):
            at = pl.ds(pl.multiple_of(i * TILE, TILE), TILE)
            out[at, cols] = jnp.dot(act[at, :], wd[:, cols], preferred_element_type=F32).astype(BF16)
            return _

        lax.fori_loop(0, tiles, project_tile, 0)

    pass_on(down_pieces[0])
    begin(down_pieces[2])
    project(0)
    pass_on(down_pieces[1])
    begin(down_pieces[3])
    send_back(0, 1, n)
    project(1)
    pass_on(down_pieces[2])
    send_back(1, 1, n)
    project(2)
    pass_on(down_pieces[3])
    for j in range(2):
        wait_rows(out, n - 1, columns_of(j), sem_back.at[0, j])
    scale = 1.0 / math.sqrt(total_tokens)
    tail_cut = 4

    def combine(h):
        for j in range(h * chunks // 2, (h + 1) * chunks // 2):
            cols = slice(j * CHUNK, (j + 1) * CHUNK)
            wait_rows(back, n - 1, cols, sem_back.at[1, j])
            both = jnp.dot(mix_ref[...], back[:, cols], preferred_element_type=F32)
            layer_out[:, cols] = hidden_ref[:, cols].astype(F32) + (both[:tok] + both[tok:])
        stat_own[h, 0] = fold(column_sums(layer_out[:, h * half : (h + 1) * half]))

    def add_statistics(h):
        slots = [s.at[h] for s in (stat_w, stat_y, stat_z)]
        return add_over_devices(1 + h, stat_own.at[h], slots)

    def write_targets(h):
        last = stat_own[h, 3]
        earlier = cached_own[3]
        w = half // tail_cut
        for j in range(h * chunks // 2, (h + 1) * chunks // 2):
            cols = slice(j * CHUNK, (j + 1) * CHUNK)
            summed = jnp.zeros((tok, CHUNK), F32)
            for layer in range(4):
                if layer < 3:
                    sums = earlier[8 * layer + j : 8 * layer + j + 1, :]
                    squares = earlier[8 * layer + 4 + j : 8 * layer + 5 + j, :]
                    values = cached_ref[layer, :, cols].astype(F32)
                else:
                    k = (j - h * chunks // 2) * (CHUNK // w)
                    sums = jnp.concatenate([last[k : k + 1], last[k + 1 : k + 2]], axis=1)
                    squares = jnp.concatenate([last[4 + k : 5 + k], last[5 + k : 6 + k]], axis=1)
                    values = layer_out[:, cols]
                mean = sums / total_tokens
                variance = squares / total_tokens - mean * mean
                summed = summed + (values - mean) * lax.rsqrt(variance + 1e-5)
            targets = (summed * 0.25).astype(BF16)
            targets_ref[:, cols] = targets
            if (j + 1) * CHUNK <= window:
                residuals[0, :, cols] = (
                    (prediction_ref[:, cols].astype(F32) - targets.astype(F32)) * scale
                ).astype(BF16)

    combine(0)
    sums = add_statistics(0)
    quarter = n // 4
    next(sums, None)
    send_back(2, 1, quarter)
    next(sums, None)
    send_back(2, quarter, 2 * quarter)
    next(sums, None)
    send_back(2, 2 * quarter, 3 * quarter)
    next(sums, None)
    write_targets(0)
    pieces = [slice(k * CHUNK, (k + 1) * CHUNK) for k in range(window // CHUNK)]
    over_x = [
        start_all(
            axes["x"],
            lambda d: residuals.at[0, :, cols],
            lambda d: residuals.at[d, :, cols],
            sem_x.at[k, 0],
            sem_x.at[k, 1],
        )
        for k, cols in enumerate(pieces)
    ]
    send_back(2, 3 * quarter, n)
    project(3)
    wait_all(students_out)
    rows = students.shape[1]
    partial = raised.at[pl.ds(0, rows), pl.ds(0, window)]
    halved = rows // 2
    other = pl.ds(pl.multiple_of((1 - c) * halved, halved), halved)
    kept = pl.ds(pl.multiple_of(c * halved, halved), halved)
    part = halved // ny
    least = part // nz

    def y_rows(d):
        return pl.ds(pl.multiple_of(lax.rem(y + d, ny) * part, part), part)

    def z_rows(d):
        return pl.ds(pl.multiple_of(lax.rem(z + d, nz) * least, least), least)

    over_c, over_y, over_z = [], [], []
    for k, cols in enumerate(pieces):
        for d in range(nx):
            if d:
                over_x[k][d - 1].wait_recv()

            def add(i, _):
                at = pl.ds(pl.multiple_of(i * 128, 128), 128)
                product = jnp.dot(
                    students[d, at, :], residuals[d, :, cols], preferred_element_type=F32
                )
                partial[at, cols] = product if d == 0 else partial[at, cols] + product
                return _

            lax.fori_loop(0, rows // 128, add, 0)
        over_c.append(
            start_all(
                axes["c"],
                lambda d: partial.at[other, cols],
                lambda d: from_c.at[:, cols],
                sem_c.at[k, 0],
                sem_c.at[k, 1],
            )
        )
        send_back(3, 2 * quarter * k + (k == 0), 2 * quarter * (k + 1))
    for k, cols in enumerate(pieces):
        wait_all(over_c[k])
        from_c[:, cols] = from_c[:, cols] + partial[kept, cols]
        over_y.append(
            start_all(
                axes["y"],
                lambda d: from_c.at[y_rows(d), cols],
                lambda d: from_y.at[d, :, cols],
                sem_y.at[k, 0],
                sem_y.at[k, 1],
            )
        )
    for k, cols in enumerate(pieces):
        wait_all(over_y[k])
        total = from_c[y_rows(0), cols]
        for d in range(1, ny):
            total = total + from_y[d, :, cols]
        from_y[0, :, cols] = total
        over_z.append(
            start_all(
                axes["z"],
                lambda d: from_y.at[0, z_rows(d), cols],
                lambda d: from_z.at[d, :, cols],
                sem_z.at[k, 0],
                sem_z.at[k, 1],
            )
        )
    combine(1)
    sums = add_statistics(1)
    for _ in range(4):
        next(sums, None)
    write_targets(1)
    for k, cols in enumerate(pieces):
        wait_all(over_z[k])
        total = from_y[0, z_rows(0), cols]
        for d in range(1, nz):
            total = total + from_z[d, :, cols]
        grad_ref[:, cols] = total
        for copy in over_x[k]:
            copy.wait_send()

    for piece in (gate_piece, up_piece, *down_pieces):
        for copy in piece:
            copy.wait_send()
    for copy in (*picks_out, *rings[0], *rings[1]):
        copy.wait_send()
    for j in range(chunks // 2, chunks):
        wait_rows(out, n - 1, slice(j * CHUNK, (j + 1) * CHUNK), sem_back.at[0, j])


def run(total_tokens, gain, router, routes, hidden_in, cached, prediction, student, wg, wu, wd):
    tok, width = hidden_in.shape
    window = prediction.shape[1]
    nx, ny, nz = lax.axis_size("seq"), NY, lax.axis_size("expert") // NY
    rows = width // nx
    hidden_units = wg.shape[1]
    pieces = window // CHUNK
    arrived = router.shape[0] * SLOTS
    chunks = width // CHUNK
    vmem = pl.BlockSpec(memory_space=pltpu.VMEM)
    hbm = pl.BlockSpec(memory_space=pl.ANY)
    dma = pltpu.SemaphoreType.DMA
    early, late = (24, width // 4), (8, width // 8)
    return pl.pallas_call(
        functools.partial(kernel, total_tokens),
        out_shape=(
            jax.ShapeDtypeStruct((tok, width), BF16),
            jax.ShapeDtypeStruct((rows // (2 * ny * nz), window), F32),
        ),
        in_specs=[vmem] * 7 + [hbm] * 3,
        out_specs=(vmem, vmem),
        scratch_shapes=[
            pltpu.VMEM((width, hidden_units), BF16),
            pltpu.VMEM((width, hidden_units), BF16),
            pltpu.VMEM((hidden_units, width), BF16),
            pltpu.VMEM((arrived, tok), BF16),
            pltpu.VMEM((2 * tok, arrived), BF16),
            pltpu.VMEM((nz, tok, width), BF16),
            pltpu.VMEM((nz, arrived // nz, tok), BF16),
            pltpu.VMEM((arrived, width), BF16),
            pltpu.VMEM((arrived, hidden_units), F32),
            pltpu.VMEM((arrived, hidden_units), F32),
            pltpu.VMEM((arrived, hidden_units), BF16),
            pltpu.VMEM((arrived, width), BF16),
            pltpu.VMEM((arrived, width), BF16),
            pltpu.VMEM((tok, width), F32),
            pltpu.VMEM((4, *early), F32),
            pltpu.VMEM((2 * nx - 1, *early), F32),
            pltpu.VMEM((ny - 1, *early), F32),
            pltpu.VMEM((nz - 1, *early), F32),
            pltpu.VMEM((2, 4, *late), F32),
            pltpu.VMEM((2, 2 * nx - 1, *late), F32),
            pltpu.VMEM((2, ny - 1, *late), F32),
            pltpu.VMEM((2, nz - 1, *late), F32),
            pltpu.VMEM((nx, rows, tok), BF16),
            pltpu.VMEM((nx, tok, window), BF16),
            pltpu.VMEM((rows // 2, window), F32),
            pltpu.VMEM((ny, rows // (2 * ny), window), F32),
            pltpu.VMEM((nz, rows // (2 * ny * nz), window), F32),
            dma((3,)),
            dma((2 + chunks, 2, 6)),
            dma((2, 2, nz - 1)),
            dma((2, nz - 1)),
            dma((2,)),
            dma((2, chunks)),
            dma((2, nx - 1)),
            dma((3, 3, 2, 7)),
            dma((pieces, 2, nx - 1)),
            dma((pieces, 2, 1)),
            dma((pieces, 2, ny - 1)),
            dma((pieces, 2, nz - 1)),
        ],
        compiler_params=pltpu.CompilerParams(
            collective_id=1, has_side_effects=True, vmem_limit_bytes=60 * 2**20
        ),
    )(gain, router, routes, hidden_in, cached, prediction, student, wg, wu, wd)


def body(
    hidden_in,
    norm_gain,
    router_weight,
    routes,
    w_gate,
    w_up,
    w_down,
    cached_layers,
    student_hidden,
    prediction,
):
    tok, width = hidden_in.shape
    nx, nz = lax.axis_size("seq"), lax.axis_size("expert") // NY
    total_tokens = tok * lax.axis_size(("expert", "seq", "dp"))
    student = (
        student_hidden.T.reshape(nz, NY, nx, 2, width // (2 * nx * NY * nz), tok)
        .transpose(2, 3, 1, 0, 4, 5)
        .reshape(nx, width // nx, tok)
    )
    return run(
        total_tokens,
        norm_gain[None],
        router_weight.T,
        routes.T,
        hidden_in,
        cached_layers,
        prediction,
        student,
        w_gate[0],
        w_up[0],
        w_down[0],
    )


def solution(mesh):
    tokens = P(("expert", "seq", "dp"), None)
    weights = P(("expert", "dp"), "seq", None)
    return jax.shard_map(
        body,
        mesh=mesh,
        in_specs=(
            tokens,
            P(),
            P(),
            tokens,
            weights,
            weights,
            weights,
            P(None, ("expert", "seq", "dp"), None),
            tokens,
            tokens,
        ),
        out_specs=(tokens, tokens),
        check_vma=False,
    )
```

```python
import functools
import math

import jax
import jax.numpy as jnp
from jax import lax
from jax.experimental import pallas as pl
from jax.experimental.pallas import tpu as pltpu
from jax.sharding import PartitionSpec as P

MESH = pl.DeviceIdType.MESH
F32, BF16 = jnp.float32, jnp.bfloat16
NY = 4


def wheel():
    e, x, c = lax.axis_index("expert"), lax.axis_index("seq"), lax.axis_index("dp")
    nx, nz = lax.axis_size("seq"), lax.axis_size("expert") // NY
    z, y = e // NY, lax.rem(e, NY)

    def to(z_, y_, x_, c_):
        return {"expert": z_ * NY + y_, "seq": x_, "dp": c_}

    def beside(q):
        return to(z, y, q // 2, lax.rem(q, 2))

    return {
        "c": (c, 2, lambda d: to(z, y, x, lax.rem(c + d, 2))),
        "w": (2 * x + c, 2 * nx, lambda d: beside(lax.rem(2 * x + c + d, 2 * nx))),
        "x": (x, nx, lambda d: to(z, y, lax.rem(x + d, nx), c)),
        "y": (y, NY, lambda d: to(z, lax.rem(y + d, NY), x, c)),
        "z": (z, nz, lambda d: to(lax.rem(z + d, nz), y, x, c)),
    }


def start_all(axis, source, target, send, recv):
    _, n, device = axis
    copies = []
    for d in range(1, n):
        copy = pltpu.make_async_remote_copy(
            src_ref=source(d),
            dst_ref=target(d),
            send_sem=send.at[d - 1],
            recv_sem=recv.at[d - 1],
            device_id=device(d),
            device_id_type=MESH,
        )
        copy.start()
        copies.append(copy)
    return copies


def wait_all(copies):
    for copy in copies:
        copy.wait()


def fold(row_list):
    w = row_list[0].shape[1] // 4
    return jnp.concatenate([r[:, i * w : (i + 1) * w] for r in row_list for i in range(4)], axis=0)


def unfold(block, row):
    return jnp.concatenate([block[4 * row + i : 4 * row + i + 1, :] for i in range(4)], axis=1)


def column_sums(values):
    return [jnp.sum(values, axis=0, keepdims=True), jnp.sum(values * values, axis=0, keepdims=True)]


SLOTS = 16
CHUNK = 512
STRIDE = 27
TILE = 256


def normalise(hidden_ref, gain_ref, router_ref):
    hidden = hidden_ref[...].astype(F32)
    mean = jnp.mean(hidden * hidden, axis=-1, keepdims=True)
    normed = (hidden * lax.rsqrt(mean + 1e-6) * gain_ref[...]).astype(BF16)
    logits = lax.dot_general(
        normed, router_ref[...], (((1,), (1,)), ((), ())), preferred_element_type=F32
    )
    return normed, logits


def choose(routes_ref, logits, pick_ref, mix_ref):
    top, tok = routes_ref.shape
    experts = logits.shape[1]

    def index(shape, dim):
        return lax.broadcasted_iota(jnp.int32, shape, dim)

    def ones(flags):
        return jnp.where(flags, 1.0, 0.0)

    names = index((experts, tok), 0)
    chosen = jnp.zeros((experts, tok), F32)
    for k in range(top):
        chosen = chosen + ones(names == routes_ref[k : k + 1, :])
    square = (tok, tok)
    earlier = ones(index(square, 0) < index(square, 1)).astype(BF16)
    place = jnp.dot(chosen.astype(BF16), earlier, preferred_element_type=F32)
    code = jnp.where(chosen > 0.5, place, -1.0).astype(BF16)
    same = ones(index(square, 0) == index(square, 1)).astype(BF16)
    code_of = lax.dot_general(same, code, (((1,), (1,)), ((), ())), preferred_element_type=F32)
    tall, wide = (experts * SLOTS, experts), (experts, experts * SLOTS)
    spread_rows = ones(index(tall, 0) // SLOTS == index(tall, 1)).astype(BF16)
    spread = ones(index(wide, 1) // SLOTS == index(wide, 0)).astype(BF16)
    rows = jnp.dot(spread_rows, code, preferred_element_type=F32)
    slots = lax.rem(index(rows.shape, 0), SLOTS).astype(F32)
    pick_ref[...] = ones(rows == slots).astype(BF16)
    affinity = jnp.where(code_of > -0.5, jax.nn.sigmoid(logits), 0.0)
    share = affinity / jnp.sum(affinity, axis=-1, keepdims=True)
    high = share.astype(BF16)
    low = (share - high.astype(F32)).astype(BF16)
    columns = jnp.dot(code_of.astype(BF16), spread, preferred_element_type=F32)
    match = columns == lax.rem(index(columns.shape, 1), SLOTS).astype(F32)
    for i, part in enumerate((high, low)):
        shares = jnp.dot(part, spread, preferred_element_type=F32)
        mix_ref[i * tok : (i + 1) * tok, :] = jnp.where(match, shares, 0.0).astype(BF16)


def kernel(
    total_tokens,
    gain_ref,
    router_ref,
    routes_ref,
    hidden_ref,
    cached_in,
    prediction_in,
    student_ref,
    wg_ref,
    wu_ref,
    wd_ref,
    targets_ref,
    grad_ref,
    wg,
    wu,
    wd,
    cached_ref,
    prediction_ref,
    pick_ref,
    mix_ref,
    blocks,
    picks,
    arrived,
    gated,
    raised,
    act,
    out,
    back,
    layer_out,
    cached_own,
    cached_w,
    cached_y,
    cached_z,
    stat_own,
    stat_w,
    stat_y,
    stat_z,
    students,
    residuals,
    from_c,
    from_y,
    from_z,
    sem_own,
    sem_w,
    sem_ring,
    sem_pick,
    sem_rows,
    sem_back,
    sem_st,
    sem_s,
    sem_x,
    sem_c,
    sem_y,
    sem_z,
):
    axes = wheel()
    tok, width = hidden_ref.shape
    window = prediction_ref.shape[1]
    e, x, c = lax.axis_index("expert"), lax.axis_index("seq"), lax.axis_index("dp")
    nx = axes["x"][1]
    n = 2 * lax.axis_size("expert")
    me = 2 * e + c
    half = width // 2
    z, nz, z_device = axes["z"]
    y, ny, _ = axes["y"]

    def peer(d):
        p = lax.rem(me + d, n)
        return p, {"expert": p // 2, "seq": x, "dp": lax.rem(p, 2)}

    barrier = pltpu.get_barrier_semaphore()

    def greet(d, _):
        pl.semaphore_signal(barrier, inc=1, device_id=peer(d)[1], device_id_type=MESH)
        return _

    lax.fori_loop(1, n, greet, 0)
    for d in range(1, 2 * nx):
        pl.semaphore_signal(barrier, inc=1, device_id=axes["w"][2](d), device_id_type=MESH)
    mine = []

    def bring(source, target):
        copy = pltpu.make_async_copy(source, target, sem_own.at[len(mine)])
        copy.start()
        mine.append(copy)

    bring(cached_in, cached_ref)
    bring(prediction_in, prediction_ref)
    bring(student_ref.at[x], students.at[0])
    for shard, whole in ((wg_ref, wg), (wu_ref, wu), (wd_ref, wd)):
        rows = shard.shape[0]
        bring(shard, whole.at[pl.ds(pl.multiple_of(x * rows, 16), rows)])
    pl.semaphore_wait(barrier, n - 1 + 2 * nx - 1)

    right, left = axes["x"][2](1), axes["x"][2](nx - 1)
    before, after = lax.rem(x + nx - 1, nx), lax.rem(x + 1, nx)

    def weight_piece(number, shard, whole, cols):
        rows = shard.shape[0]
        cut = rows // 2

        def at(origin, part):
            return pl.ds(pl.multiple_of(origin * rows + part * cut, 16), cut)

        def copy(i, source, origin, part, device):
            return pltpu.make_async_remote_copy(
                src_ref=source,
                dst_ref=whole.at[at(origin, part), cols],
                send_sem=sem_w.at[number, 0, i],
                recv_sem=sem_w.at[number, 1, i],
                device_id=device,
                device_id_type=MESH,
            )

        def own(part):
            return shard.at[pl.ds(part * cut, cut), cols]

        def passed(origin, part):
            return whole.at[at(origin, part), cols]

        return [
            copy(0, own(0), x, 0, right),
            copy(1, own(1), x, 1, right),
            copy(2, own(1), x, 1, left),
            copy(3, own(0), x, 0, left),
            copy(4, passed(before, 0), before, 0, right),
            copy(5, passed(after, 1), after, 1, left),
        ]

    def begin(piece):
        for i in (0, 2, 1, 3):
            piece[i].start()

    def pass_on(piece):
        piece[0].wait_recv()
        piece[4].start()
        piece[2].wait_recv()
        piece[5].start()

    every = slice(0, wg.shape[1])
    gate_piece = weight_piece(0, wg_ref, wg, every)
    up_piece = weight_piece(1, wu_ref, wu, every)
    chunks = width // CHUNK
    down_pieces = [
        weight_piece(2 + i, wd_ref, wd, slice(i * CHUNK, (i + 1) * CHUNK)) for i in range(chunks)
    ]
    begin(gate_piece)
    blocks[z], logits = normalise(hidden_ref, gain_ref, router_ref)
    choose(routes_ref, logits, pick_ref, mix_ref)

    def block(p):
        return pl.ds(pl.multiple_of(p * SLOTS, SLOTS), SLOTS)

    def scatter(source, target, cols, send, recv, first, end):
        def go(i, _):
            p, device = peer(lax.rem(i * STRIDE, n))
            pltpu.make_async_remote_copy(
                src_ref=source.at[block(p), cols],
                dst_ref=target.at[block(me), cols],
                send_sem=send,
                recv_sem=recv,
                device_id=device,
                device_id_type=MESH,
            ).start()
            return _

        lax.fori_loop(first, end, go, 0)
        if first == 1:
            target[block(me), cols] = source[block(me), cols]

    def wait_rows(ref, count, cols, sem):
        rows = ref.at[pl.ds(0, count * SLOTS), cols]
        pltpu.make_async_copy(rows, rows, sem).wait()

    group = 2 * ny * SLOTS
    half_block = tok // 2
    last = nz - 2

    def ring(way, m):
        s, part = m // 2, (m + way) % 2
        b = lax.rem(z + (nz - s if way == 0 else s), nz)
        rows = blocks.at[b, pl.ds(part * half_block, half_block)]
        return pltpu.make_async_remote_copy(
            src_ref=rows,
            dst_ref=rows,
            send_sem=sem_ring.at[0, way, m],
            recv_sem=sem_ring.at[1, way, m],
            device_id=z_device(1 if way == 0 else nz - 1),
            device_id_type=MESH,
        )

    rings = [[ring(way, m) for m in range(last + 1)] for way in range(2)]

    def group_rows(b):
        return pl.ds(pl.multiple_of(b * group, group), group)

    def start_ring(m):
        for way in range(2):
            rings[way][m].start()

    def next_ring(m):
        for way in range(2):
            rings[way][m].wait_recv()
            if m + 2 <= last:
                rings[way][m + 2].start()

    def select(b):
        for j in range(chunks):
            cols = slice(j * CHUNK, (j + 1) * CHUNK)
            out[group_rows(b), cols] = jnp.dot(
                picks[b], blocks[b, :, cols], preferred_element_type=F32
            ).astype(BF16)
        p = (b * ny + y) * 2 + c

        def go(d, _):
            q = lax.rem(2 * y + c + d, 2 * ny)
            pltpu.make_async_remote_copy(
                src_ref=out.at[block(b * 2 * ny + q)],
                dst_ref=arrived.at[block(p)],
                send_sem=sem_rows.at[0],
                recv_sem=sem_rows.at[1],
                device_id={"expert": z * ny + q // 2, "seq": x, "dp": lax.rem(q, 2)},
                device_id_type=MESH,
            ).start()
            return _

        lax.fori_loop(1, 2 * ny, go, 0)
        arrived[block(p), :] = out[block(b * 2 * ny + 2 * y + c), :]

    picks_out = start_all(
        axes["z"],
        lambda d: pick_ref.at[group_rows(lax.rem(z + d, nz))],
        lambda d: picks.at[z],
        sem_pick.at[0],
        sem_pick.at[1],
    )
    start_ring(0)
    start_ring(1)
    picks[z] = pick_ref[group_rows(z), :]
    students_out = start_all(
        axes["x"],
        lambda d: student_ref.at[lax.rem(x + d, nx)],
        lambda d: students.at[d],
        sem_st.at[0],
        sem_st.at[1],
    )

    def add_over_devices(number, own, slots):
        for i, name in enumerate("wyz"):
            copies = start_all(
                axes[name],
                lambda d: own.at[i],
                lambda d: slots[i].at[d - 1],
                sem_s.at[number, i, 0],
                sem_s.at[number, i, 1],
            )
            yield
            wait_all(copies)
            total = own[i]
            for d in range(1, axes[name][1]):
                total = total + slots[i][d - 1]
            own[i + 1] = total

    mine[0].wait()
    stats = []
    for layer in range(3):
        stats += column_sums(cached_ref[layer].astype(F32))
    cached_own[0] = fold(stats)

    for copy in picks_out:
        copy.wait_recv()
    select(z)
    next_ring(0)
    next_ring(1)
    select(lax.rem(z + nz - 1, nz))
    select(lax.rem(z + 1, nz))
    pass_on(gate_piece)
    next_ring(2)
    next_ring(3)
    select(lax.rem(z + nz - 2, nz))
    select(lax.rem(z + 2, nz))
    next_ring(4)
    next_ring(5)
    gate_piece[1].wait_recv()
    gate_piece[3].wait_recv()
    begin(up_piece)
    select(lax.rem(z + nz - 3, nz))
    select(lax.rem(z + 3, nz))
    next_ring(6)
    select(lax.rem(z + nz // 2, nz))
    cached_sums = add_over_devices(0, cached_own, (cached_w, cached_y, cached_z))
    next(cached_sums, None)
    for copy in mine[1:]:
        copy.wait()
    gate_piece[4].wait_recv()
    gate_piece[5].wait_recv()
    pass_on(up_piece)
    everything = slice(0, width)
    wait_rows(arrived, n - nz, everything, sem_rows.at[1])

    def gate_tile(i, _):
        at = pl.ds(pl.multiple_of(i * TILE, TILE), TILE)
        gate = jnp.dot(arrived[at, :], wg[...], preferred_element_type=F32)
        gated[at, :] = gate * jax.nn.sigmoid(gate)
        return _

    shard = wu_ref.shape[0]

    def up_part(at, origin):
        rows = pl.ds(pl.multiple_of(origin * shard, shard), shard)
        return jnp.dot(arrived[at, rows], wu[rows, :], preferred_element_type=F32)

    def up_tile(i, _):
        at = pl.ds(pl.multiple_of(i * TILE, TILE), TILE)
        raised[at, :] = up_part(at, x) + up_part(at, before) + up_part(at, after)
        return _

    def act_tile(i, _):
        at = pl.ds(pl.multiple_of(i * TILE, TILE), TILE)
        up = raised[at, :] + up_part(at, lax.rem(x + 2, nx))
        act[at, :] = (gated[at, :] * up).astype(BF16)
        return _

    tiles = arrived.shape[0] // TILE
    next(cached_sums, None)
    lax.fori_loop(0, tiles, gate_tile, 0)
    next(cached_sums, None)
    up_piece[1].wait_recv()
    up_piece[3].wait_recv()
    begin(down_pieces[0])
    lax.fori_loop(0, tiles, up_tile, 0)
    next(cached_sums, None)
    up_piece[4].wait_recv()
    up_piece[5].wait_recv()
    begin(down_pieces[1])
    lax.fori_loop(0, tiles, act_tile, 0)
    wait_rows(out, n - nz, everything, sem_rows.at[0])

    def columns_of(j):
        return slice(j * CHUNK, (j + 1) * CHUNK)

    def send_back(j, first, end):
        scatter(out, back, columns_of(j), sem_back.at[0, j], sem_back.at[1, j], first, end)

    def project(j):
        for i in (1, 3, 4, 5):
            down_pieces[j][i].wait_recv()
        cols = columns_of(j)

        def project_tile(i, _):
            at = pl.ds(pl.multiple_of(i * TILE, TILE), TILE)
            out[at, cols] = jnp.dot(act[at, :], wd[:, cols], preferred_element_type=F32).astype(BF16)
            return _

        lax.fori_loop(0, tiles, project_tile, 0)

    pass_on(down_pieces[0])
    begin(down_pieces[2])
    project(0)
    pass_on(down_pieces[1])
    begin(down_pieces[3])
    send_back(0, 1, n)
    project(1)
    pass_on(down_pieces[2])
    send_back(1, 1, n)
    project(2)
    pass_on(down_pieces[3])
    for j in range(2):
        wait_rows(out, n - 1, columns_of(j), sem_back.at[0, j])
    scale = 1.0 / math.sqrt(total_tokens)
    tail_cut = 4

    def combine(h):
        for j in range(h * chunks // 2, (h + 1) * chunks // 2):
            cols = slice(j * CHUNK, (j + 1) * CHUNK)
            wait_rows(back, n - 1, cols, sem_back.at[1, j])
            both = jnp.dot(mix_ref[...], back[:, cols], preferred_element_type=F32)
            layer_out[:, cols] = hidden_ref[:, cols].astype(F32) + (both[:tok] + both[tok:])
        stat_own[h, 0] = fold(column_sums(layer_out[:, h * half : (h + 1) * half]))

    def add_statistics(h):
        slots = [s.at[h] for s in (stat_w, stat_y, stat_z)]
        return add_over_devices(1 + h, stat_own.at[h], slots)

    def write_targets(h):
        last = stat_own[h, 3]
        earlier = cached_own[3]
        w = half // tail_cut
        for j in range(h * chunks // 2, (h + 1) * chunks // 2):
            cols = slice(j * CHUNK, (j + 1) * CHUNK)
            summed = jnp.zeros((tok, CHUNK), F32)
            for layer in range(4):
                if layer < 3:
                    sums = earlier[8 * layer + j : 8 * layer + j + 1, :]
                    squares = earlier[8 * layer + 4 + j : 8 * layer + 5 + j, :]
                    values = cached_ref[layer, :, cols].astype(F32)
                else:
                    k = (j - h * chunks // 2) * (CHUNK // w)
                    sums = jnp.concatenate([last[k : k + 1], last[k + 1 : k + 2]], axis=1)
                    squares = jnp.concatenate([last[4 + k : 5 + k], last[5 + k : 6 + k]], axis=1)
                    values = layer_out[:, cols]
                mean = sums / total_tokens
                variance = squares / total_tokens - mean * mean
                summed = summed + (values - mean) * lax.rsqrt(variance + 1e-5)
            targets = (summed * 0.25).astype(BF16)
            targets_ref[:, cols] = targets
            if (j + 1) * CHUNK <= window:
                residuals[0, :, cols] = (
                    (prediction_ref[:, cols].astype(F32) - targets.astype(F32)) * scale
                ).astype(BF16)

    send_back(2, 1, 20)
    combine(0)
    sums = add_statistics(0)
    next(sums, None)
    send_back(2, 20, 28)
    next(sums, None)
    send_back(2, 28, 36)
    next(sums, None)
    send_back(2, 36, 44)
    next(sums, None)
    write_targets(0)
    pieces = [slice(k * CHUNK, (k + 1) * CHUNK) for k in range(window // CHUNK)]
    over_x = [
        start_all(
            axes["x"],
            lambda d: residuals.at[0, :, cols],
            lambda d: residuals.at[d, :, cols],
            sem_x.at[k, 0],
            sem_x.at[k, 1],
        )
        for k, cols in enumerate(pieces)
    ]
    send_back(2, 44, n)
    project(3)
    send_back(3, 1, 20)
    wait_all(students_out)
    rows = students.shape[1]
    partial = raised.at[pl.ds(0, rows), pl.ds(0, window)]
    halved = rows // 2
    other = pl.ds(pl.multiple_of((1 - c) * halved, halved), halved)
    kept = pl.ds(pl.multiple_of(c * halved, halved), halved)
    part = halved // ny
    least = part // nz

    def y_rows(d):
        return pl.ds(pl.multiple_of(lax.rem(y + d, ny) * part, part), part)

    def z_rows(d):
        return pl.ds(pl.multiple_of(lax.rem(z + d, nz) * least, least), least)

    over_c, over_y, over_z = [], [], []
    for k, cols in enumerate(pieces):
        for d in range(nx):
            if d:
                over_x[k][d - 1].wait_recv()

            def add(i, _):
                at = pl.ds(pl.multiple_of(i * 128, 128), 128)
                product = jnp.dot(
                    students[d, at, :], residuals[d, :, cols], preferred_element_type=F32
                )
                partial[at, cols] = product if d == 0 else partial[at, cols] + product
                return _

            lax.fori_loop(0, rows // 128, add, 0)
        over_c.append(
            start_all(
                axes["c"],
                lambda d: partial.at[other, cols],
                lambda d: from_c.at[:, cols],
                sem_c.at[k, 0],
                sem_c.at[k, 1],
            )
        )
        send_back(3, (20, 42)[k], (42, n)[k])
    for k, cols in enumerate(pieces):
        wait_all(over_c[k])
        from_c[:, cols] = from_c[:, cols] + partial[kept, cols]
        over_y.append(
            start_all(
                axes["y"],
                lambda d: from_c.at[y_rows(d), cols],
                lambda d: from_y.at[d, :, cols],
                sem_y.at[k, 0],
                sem_y.at[k, 1],
            )
        )
    for k, cols in enumerate(pieces):
        wait_all(over_y[k])
        total = from_c[y_rows(0), cols]
        for d in range(1, ny):
            total = total + from_y[d, :, cols]
        from_y[0, :, cols] = total
        over_z.append(
            start_all(
                axes["z"],
                lambda d: from_y.at[0, z_rows(d), cols],
                lambda d: from_z.at[d, :, cols],
                sem_z.at[k, 0],
                sem_z.at[k, 1],
            )
        )
    combine(1)
    sums = add_statistics(1)
    for _ in range(4):
        next(sums, None)
    write_targets(1)
    for k, cols in enumerate(pieces):
        wait_all(over_z[k])
        total = from_y[0, z_rows(0), cols]
        for d in range(1, nz):
            total = total + from_z[d, :, cols]
        grad_ref[:, cols] = total
        for copy in over_x[k]:
            copy.wait_send()

    for piece in (gate_piece, up_piece, *down_pieces):
        for copy in piece:
            copy.wait_send()
    for copy in (*picks_out, *rings[0], *rings[1]):
        copy.wait_send()
    for j in range(chunks // 2, chunks):
        wait_rows(out, n - 1, slice(j * CHUNK, (j + 1) * CHUNK), sem_back.at[0, j])


def run(total_tokens, gain, router, routes, hidden_in, cached, prediction, student, wg, wu, wd):
    tok, width = hidden_in.shape
    window = prediction.shape[1]
    nx, ny, nz = lax.axis_size("seq"), NY, lax.axis_size("expert") // NY
    rows = width // nx
    hidden_units = wg.shape[1]
    pieces = window // CHUNK
    arrived = router.shape[0] * SLOTS
    chunks = width // CHUNK
    vmem = pl.BlockSpec(memory_space=pltpu.VMEM)
    hbm = pl.BlockSpec(memory_space=pl.ANY)
    dma = pltpu.SemaphoreType.DMA
    early, late = (24, width // 4), (8, width // 8)
    return pl.pallas_call(
        functools.partial(kernel, total_tokens),
        out_shape=(
            jax.ShapeDtypeStruct((tok, width), BF16),
            jax.ShapeDtypeStruct((rows // (2 * ny * nz), window), F32),
        ),
        in_specs=[vmem] * 4 + [hbm] * 6,
        out_specs=(vmem, vmem),
        scratch_shapes=[
            pltpu.VMEM((width, hidden_units), BF16),
            pltpu.VMEM((width, hidden_units), BF16),
            pltpu.VMEM((hidden_units, width), BF16),
            pltpu.VMEM(cached.shape, BF16),
            pltpu.VMEM(prediction.shape, BF16),
            pltpu.VMEM((arrived, tok), BF16),
            pltpu.VMEM((2 * tok, arrived), BF16),
            pltpu.VMEM((nz, tok, width), BF16),
            pltpu.VMEM((nz, arrived // nz, tok), BF16),
            pltpu.VMEM((arrived, width), BF16),
            pltpu.VMEM((arrived, hidden_units), F32),
            pltpu.VMEM((arrived, hidden_units), F32),
            pltpu.VMEM((arrived, hidden_units), BF16),
            pltpu.VMEM((arrived, width), BF16),
            pltpu.VMEM((arrived, width), BF16),
            pltpu.VMEM((tok, width), F32),
            pltpu.VMEM((4, *early), F32),
            pltpu.VMEM((2 * nx - 1, *early), F32),
            pltpu.VMEM((ny - 1, *early), F32),
            pltpu.VMEM((nz - 1, *early), F32),
            pltpu.VMEM((2, 4, *late), F32),
            pltpu.VMEM((2, 2 * nx - 1, *late), F32),
            pltpu.VMEM((2, ny - 1, *late), F32),
            pltpu.VMEM((2, nz - 1, *late), F32),
            pltpu.VMEM((nx, rows, tok), BF16),
            pltpu.VMEM((nx, tok, window), BF16),
            pltpu.VMEM((rows // 2, window), F32),
            pltpu.VMEM((ny, rows // (2 * ny), window), F32),
            pltpu.VMEM((nz, rows // (2 * ny * nz), window), F32),
            dma((6,)),
            dma((2 + chunks, 2, 6)),
            dma((2, 2, nz - 1)),
            dma((2, nz - 1)),
            dma((2,)),
            dma((2, chunks)),
            dma((2, nx - 1)),
            dma((3, 3, 2, 7)),
            dma((pieces, 2, nx - 1)),
            dma((pieces, 2, 1)),
            dma((pieces, 2, ny - 1)),
            dma((pieces, 2, nz - 1)),
        ],
        compiler_params=pltpu.CompilerParams(
            collective_id=1, has_side_effects=True, vmem_limit_bytes=60 * 2**20
        ),
    )(gain, router, routes, hidden_in, cached, prediction, student, wg, wu, wd)


def body(
    hidden_in,
    norm_gain,
    router_weight,
    routes,
    w_gate,
    w_up,
    w_down,
    cached_layers,
    student_hidden,
    prediction,
):
    tok, width = hidden_in.shape
    nx, nz = lax.axis_size("seq"), lax.axis_size("expert") // NY
    total_tokens = tok * lax.axis_size(("expert", "seq", "dp"))
    student = (
        student_hidden.T.reshape(nz, NY, nx, 2, width // (2 * nx * NY * nz), tok)
        .transpose(2, 3, 1, 0, 4, 5)
        .reshape(nx, width // nx, tok)
    )
    return run(
        total_tokens,
        norm_gain[None],
        router_weight.T,
        routes.T,
        hidden_in,
        cached_layers,
        prediction,
        student,
        w_gate[0],
        w_up[0],
        w_down[0],
    )


def solution(mesh):
    tokens = P(("expert", "seq", "dp"), None)
    weights = P(("expert", "dp"), "seq", None)
    return jax.shard_map(
        body,
        mesh=mesh,
        in_specs=(
            tokens,
            P(),
            P(),
            tokens,
            weights,
            weights,
            weights,
            P(None, ("expert", "seq", "dp"), None),
            tokens,
            tokens,
        ),
        out_specs=(tokens, tokens),
        check_vma=False,
    )
```

```python
import functools
import math

import jax
import jax.numpy as jnp
from jax import lax
from jax.experimental import pallas as pl
from jax.experimental.pallas import tpu as pltpu
from jax.sharding import PartitionSpec as P

MESH = pl.DeviceIdType.MESH
F32, BF16 = jnp.float32, jnp.bfloat16
NY = 4


def wheel():
    e, x, c = lax.axis_index("expert"), lax.axis_index("seq"), lax.axis_index("dp")
    nx, nz = lax.axis_size("seq"), lax.axis_size("expert") // NY
    z, y = e // NY, lax.rem(e, NY)

    def to(z_, y_, x_, c_):
        return {"expert": z_ * NY + y_, "seq": x_, "dp": c_}

    def beside(q):
        return to(z, y, q // 2, lax.rem(q, 2))

    return {
        "c": (c, 2, lambda d: to(z, y, x, lax.rem(c + d, 2))),
        "w": (2 * x + c, 2 * nx, lambda d: beside(lax.rem(2 * x + c + d, 2 * nx))),
        "x": (x, nx, lambda d: to(z, y, lax.rem(x + d, nx), c)),
        "y": (y, NY, lambda d: to(z, lax.rem(y + d, NY), x, c)),
        "z": (z, nz, lambda d: to(lax.rem(z + d, nz), y, x, c)),
    }


def start_all(axis, source, target, send, recv):
    _, n, device = axis
    copies = []
    for d in range(1, n):
        copy = pltpu.make_async_remote_copy(
            src_ref=source(d),
            dst_ref=target(d),
            send_sem=send.at[d - 1],
            recv_sem=recv.at[d - 1],
            device_id=device(d),
            device_id_type=MESH,
        )
        copy.start()
        copies.append(copy)
    return copies


def wait_all(copies):
    for copy in copies:
        copy.wait()


def fold(row_list):
    w = row_list[0].shape[1] // 4
    return jnp.concatenate([r[:, i * w : (i + 1) * w] for r in row_list for i in range(4)], axis=0)


def unfold(block, row):
    return jnp.concatenate([block[4 * row + i : 4 * row + i + 1, :] for i in range(4)], axis=1)


def column_sums(values):
    return [jnp.sum(values, axis=0, keepdims=True), jnp.sum(values * values, axis=0, keepdims=True)]


SLOTS = 16
CHUNK = 512
STRIDE = 27
TILE = 256


def normalise(hidden_ref, gain_ref, router_ref):
    hidden = hidden_ref[...].astype(F32)
    mean = jnp.mean(hidden * hidden, axis=-1, keepdims=True)
    normed = (hidden * lax.rsqrt(mean + 1e-6) * gain_ref[...]).astype(BF16)
    logits = lax.dot_general(
        normed, router_ref[...], (((1,), (1,)), ((), ())), preferred_element_type=F32
    )
    return normed, logits


def choose(routes_ref, logits, pick_ref, mix_ref):
    top, tok = routes_ref.shape
    experts = logits.shape[1]

    def index(shape, dim):
        return lax.broadcasted_iota(jnp.int32, shape, dim)

    def ones(flags):
        return jnp.where(flags, 1.0, 0.0)

    names = index((experts, tok), 0)
    chosen = jnp.zeros((experts, tok), F32)
    for k in range(top):
        chosen = chosen + ones(names == routes_ref[k : k + 1, :])
    square = (tok, tok)
    earlier = ones(index(square, 0) < index(square, 1)).astype(BF16)
    place = jnp.dot(chosen.astype(BF16), earlier, preferred_element_type=F32)
    code = jnp.where(chosen > 0.5, place, -1.0).astype(BF16)
    same = ones(index(square, 0) == index(square, 1)).astype(BF16)
    code_of = lax.dot_general(same, code, (((1,), (1,)), ((), ())), preferred_element_type=F32)
    tall, wide = (experts * SLOTS, experts), (experts, experts * SLOTS)
    spread_rows = ones(index(tall, 0) // SLOTS == index(tall, 1)).astype(BF16)
    spread = ones(index(wide, 1) // SLOTS == index(wide, 0)).astype(BF16)
    rows = jnp.dot(spread_rows, code, preferred_element_type=F32)
    slots = lax.rem(index(rows.shape, 0), SLOTS).astype(F32)
    pick_ref[...] = ones(rows == slots).astype(BF16)
    affinity = jnp.where(code_of > -0.5, jax.nn.sigmoid(logits), 0.0)
    share = affinity / jnp.sum(affinity, axis=-1, keepdims=True)
    high = share.astype(BF16)
    low = (share - high.astype(F32)).astype(BF16)
    columns = jnp.dot(code_of.astype(BF16), spread, preferred_element_type=F32)
    match = columns == lax.rem(index(columns.shape, 1), SLOTS).astype(F32)
    for i, part in enumerate((high, low)):
        shares = jnp.dot(part, spread, preferred_element_type=F32)
        mix_ref[i * tok : (i + 1) * tok, :] = jnp.where(match, shares, 0.0).astype(BF16)


def kernel(
    total_tokens,
    gain_ref,
    router_ref,
    routes_ref,
    hidden_ref,
    cached_in,
    prediction_in,
    student_ref,
    wg_ref,
    wu_ref,
    wd_ref,
    targets_ref,
    grad_ref,
    wg,
    wu,
    wd,
    cached_ref,
    prediction_ref,
    pick_ref,
    mix_ref,
    blocks,
    picks,
    arrived,
    gated,
    raised,
    act,
    out,
    back,
    layer_out,
    cached_own,
    cached_w,
    cached_y,
    cached_z,
    stat_own,
    stat_w,
    stat_y,
    stat_z,
    students,
    residuals,
    from_c,
    from_y,
    from_z,
    sem_own,
    sem_w,
    sem_ring,
    sem_pick,
    sem_rows,
    sem_back,
    sem_st,
    sem_s,
    sem_x,
    sem_c,
    sem_y,
    sem_z,
):
    axes = wheel()
    tok, width = hidden_ref.shape
    window = prediction_ref.shape[1]
    e, x, c = lax.axis_index("expert"), lax.axis_index("seq"), lax.axis_index("dp")
    nx = axes["x"][1]
    n = 2 * lax.axis_size("expert")
    me = 2 * e + c
    half = width // 2
    z, nz, z_device = axes["z"]
    y, ny, _ = axes["y"]

    def peer(d):
        p = lax.rem(me + d, n)
        return p, {"expert": p // 2, "seq": x, "dp": lax.rem(p, 2)}

    barrier = pltpu.get_barrier_semaphore()

    def greet(d, _):
        pl.semaphore_signal(barrier, inc=1, device_id=peer(d)[1], device_id_type=MESH)
        return _

    lax.fori_loop(1, n, greet, 0)
    for d in range(1, 2 * nx):
        pl.semaphore_signal(barrier, inc=1, device_id=axes["w"][2](d), device_id_type=MESH)
    mine = []

    def bring(source, target):
        copy = pltpu.make_async_copy(source, target, sem_own.at[len(mine)])
        copy.start()
        mine.append(copy)

    bring(cached_in, cached_ref)
    bring(prediction_in, prediction_ref)
    bring(student_ref.at[x], students.at[0])
    for shard, whole in ((wg_ref, wg), (wu_ref, wu), (wd_ref, wd)):
        rows = shard.shape[0]
        bring(shard, whole.at[pl.ds(pl.multiple_of(x * rows, 16), rows)])
    pl.semaphore_wait(barrier, n - 1 + 2 * nx - 1)

    right, left = axes["x"][2](1), axes["x"][2](nx - 1)
    before, after = lax.rem(x + nx - 1, nx), lax.rem(x + 1, nx)

    def weight_piece(number, shard, whole, cols):
        rows = shard.shape[0]
        cut = rows // 2

        def at(origin, part):
            return pl.ds(pl.multiple_of(origin * rows + part * cut, 16), cut)

        def copy(i, source, origin, part, device):
            return pltpu.make_async_remote_copy(
                src_ref=source,
                dst_ref=whole.at[at(origin, part), cols],
                send_sem=sem_w.at[number, 0, i],
                recv_sem=sem_w.at[number, 1, i],
                device_id=device,
                device_id_type=MESH,
            )

        def own(part):
            return shard.at[pl.ds(part * cut, cut), cols]

        def passed(origin, part):
            return whole.at[at(origin, part), cols]

        return [
            copy(0, own(0), x, 0, right),
            copy(1, own(1), x, 1, right),
            copy(2, own(1), x, 1, left),
            copy(3, own(0), x, 0, left),
            copy(4, passed(before, 0), before, 0, right),
            copy(5, passed(after, 1), after, 1, left),
        ]

    def begin(piece):
        for i in (0, 2, 1, 3):
            piece[i].start()

    def pass_on(piece):
        piece[0].wait_recv()
        piece[4].start()
        piece[2].wait_recv()
        piece[5].start()

    every = slice(0, wg.shape[1])
    gate_piece = weight_piece(0, wg_ref, wg, every)
    up_piece = weight_piece(1, wu_ref, wu, every)
    chunks = width // CHUNK
    down_pieces = [
        weight_piece(2 + i, wd_ref, wd, slice(i * CHUNK, (i + 1) * CHUNK)) for i in range(chunks)
    ]
    begin(gate_piece)
    blocks[z], logits = normalise(hidden_ref, gain_ref, router_ref)
    choose(routes_ref, logits, pick_ref, mix_ref)

    def block(p):
        return pl.ds(pl.multiple_of(p * SLOTS, SLOTS), SLOTS)

    def scatter(source, target, cols, send, recv, first, end):
        def go(i, _):
            p, device = peer(lax.rem(i * STRIDE, n))
            pltpu.make_async_remote_copy(
                src_ref=source.at[block(p), cols],
                dst_ref=target.at[block(me), cols],
                send_sem=send,
                recv_sem=recv,
                device_id=device,
                device_id_type=MESH,
            ).start()
            return _

        lax.fori_loop(first, end, go, 0)
        if first == 1:
            target[block(me), cols] = source[block(me), cols]

    def wait_rows(ref, count, cols, sem):
        rows = ref.at[pl.ds(0, count * SLOTS), cols]
        pltpu.make_async_copy(rows, rows, sem).wait()

    group = 2 * ny * SLOTS
    half_block = tok // 2
    last = nz - 2

    def ring(way, m):
        s, part = m // 2, (m + way) % 2
        b = lax.rem(z + (nz - s if way == 0 else s), nz)
        rows = blocks.at[b, pl.ds(part * half_block, half_block)]
        return pltpu.make_async_remote_copy(
            src_ref=rows,
            dst_ref=rows,
            send_sem=sem_ring.at[0, way, m],
            recv_sem=sem_ring.at[1, way, m],
            device_id=z_device(1 if way == 0 else nz - 1),
            device_id_type=MESH,
        )

    rings = [[ring(way, m) for m in range(last + 1)] for way in range(2)]

    def group_rows(b):
        return pl.ds(pl.multiple_of(b * group, group), group)

    def start_ring(m):
        for way in range(2):
            rings[way][m].start()

    def next_ring(m):
        for way in range(2):
            rings[way][m].wait_recv()
            if m + 2 <= last:
                rings[way][m + 2].start()

    def select(b):
        for j in range(chunks):
            cols = slice(j * CHUNK, (j + 1) * CHUNK)
            out[group_rows(b), cols] = jnp.dot(
                picks[b], blocks[b, :, cols], preferred_element_type=F32
            ).astype(BF16)
        p = (b * ny + y) * 2 + c

        def go(d, _):
            q = lax.rem(2 * y + c + d, 2 * ny)
            pltpu.make_async_remote_copy(
                src_ref=out.at[block(b * 2 * ny + q)],
                dst_ref=arrived.at[block(p)],
                send_sem=sem_rows.at[0],
                recv_sem=sem_rows.at[1],
                device_id={"expert": z * ny + q // 2, "seq": x, "dp": lax.rem(q, 2)},
                device_id_type=MESH,
            ).start()
            return _

        lax.fori_loop(1, 2 * ny, go, 0)
        arrived[block(p), :] = out[block(b * 2 * ny + 2 * y + c), :]

    picks_out = start_all(
        axes["z"],
        lambda d: pick_ref.at[group_rows(lax.rem(z + d, nz))],
        lambda d: picks.at[z],
        sem_pick.at[0],
        sem_pick.at[1],
    )
    start_ring(0)
    start_ring(1)
    picks[z] = pick_ref[group_rows(z), :]
    students_out = start_all(
        axes["x"],
        lambda d: student_ref.at[lax.rem(x + d, nx)],
        lambda d: students.at[d],
        sem_st.at[0],
        sem_st.at[1],
    )

    def add_over_devices(number, own, slots):
        for i, name in enumerate("wyz"):
            copies = start_all(
                axes[name],
                lambda d: own.at[i],
                lambda d: slots[i].at[d - 1],
                sem_s.at[number, i, 0],
                sem_s.at[number, i, 1],
            )
            yield
            wait_all(copies)
            total = own[i]
            for d in range(1, axes[name][1]):
                total = total + slots[i][d - 1]
            own[i + 1] = total

    mine[0].wait()
    stats = []
    for layer in range(3):
        stats += column_sums(cached_ref[layer].astype(F32))
    cached_own[0] = fold(stats)

    for copy in picks_out:
        copy.wait_recv()
    select(z)
    next_ring(0)
    next_ring(1)
    select(lax.rem(z + nz - 1, nz))
    select(lax.rem(z + 1, nz))
    pass_on(gate_piece)
    next_ring(2)
    next_ring(3)
    select(lax.rem(z + nz - 2, nz))
    select(lax.rem(z + 2, nz))
    next_ring(4)
    next_ring(5)
    gate_piece[1].wait_recv()
    gate_piece[3].wait_recv()
    begin(up_piece)
    select(lax.rem(z + nz - 3, nz))
    select(lax.rem(z + 3, nz))
    next_ring(6)
    select(lax.rem(z + nz // 2, nz))
    cached_sums = add_over_devices(0, cached_own, (cached_w, cached_y, cached_z))
    next(cached_sums, None)
    for copy in mine[1:]:
        copy.wait()
    gate_piece[4].wait_recv()
    gate_piece[5].wait_recv()
    pass_on(up_piece)
    everything = slice(0, width)
    wait_rows(arrived, n - nz, everything, sem_rows.at[1])

    def gate_tile(i, _):
        at = pl.ds(pl.multiple_of(i * TILE, TILE), TILE)
        gate = jnp.dot(arrived[at, :], wg[...], preferred_element_type=F32)
        gated[at, :] = gate * jax.nn.sigmoid(gate)
        return _

    shard = wu_ref.shape[0]

    def up_part(at, origin):
        rows = pl.ds(pl.multiple_of(origin * shard, shard), shard)
        return jnp.dot(arrived[at, rows], wu[rows, :], preferred_element_type=F32)

    def up_tile(i, _):
        at = pl.ds(pl.multiple_of(i * TILE, TILE), TILE)
        raised[at, :] = up_part(at, x) + up_part(at, before) + up_part(at, after)
        return _

    def act_tile(i, _):
        at = pl.ds(pl.multiple_of(i * TILE, TILE), TILE)
        up = raised[at, :] + up_part(at, lax.rem(x + 2, nx))
        act[at, :] = (gated[at, :] * up).astype(BF16)
        return _

    tiles = arrived.shape[0] // TILE
    next(cached_sums, None)
    lax.fori_loop(0, tiles, gate_tile, 0)
    next(cached_sums, None)
    up_piece[1].wait_recv()
    up_piece[3].wait_recv()
    begin(down_pieces[0])
    lax.fori_loop(0, tiles, up_tile, 0)
    next(cached_sums, None)
    up_piece[4].wait_recv()
    up_piece[5].wait_recv()
    begin(down_pieces[1])
    lax.fori_loop(0, tiles, act_tile, 0)
    wait_rows(out, n - nz, everything, sem_rows.at[0])

    def columns_of(j):
        return slice(j * CHUNK, (j + 1) * CHUNK)

    def send_back(j, first, end):
        scatter(out, back, columns_of(j), sem_back.at[0, j], sem_back.at[1, j], first, end)

    def project(j):
        for i in (1, 3, 4, 5):
            down_pieces[j][i].wait_recv()
        cols = columns_of(j)

        def project_tile(i, _):
            at = pl.ds(pl.multiple_of(i * TILE, TILE), TILE)
            out[at, cols] = jnp.dot(act[at, :], wd[:, cols], preferred_element_type=F32).astype(BF16)
            return _

        lax.fori_loop(0, tiles, project_tile, 0)

    pass_on(down_pieces[0])
    begin(down_pieces[2])
    project(0)
    pass_on(down_pieces[1])
    begin(down_pieces[3])
    send_back(0, 1, n)
    project(1)
    send_back(1, 1, n)
    pass_on(down_pieces[2])
    project(2)
    pass_on(down_pieces[3])
    for j in range(2):
        wait_rows(out, n - 1, columns_of(j), sem_back.at[0, j])
    scale = 1.0 / math.sqrt(total_tokens)
    tail_cut = 4

    def combine(h):
        for j in range(h * chunks // 2, (h + 1) * chunks // 2):
            cols = slice(j * CHUNK, (j + 1) * CHUNK)
            wait_rows(back, n - 1, cols, sem_back.at[1, j])
            both = jnp.dot(mix_ref[...], back[:, cols], preferred_element_type=F32)
            layer_out[:, cols] = hidden_ref[:, cols].astype(F32) + (both[:tok] + both[tok:])
        stat_own[h, 0] = fold(column_sums(layer_out[:, h * half : (h + 1) * half]))

    def add_statistics(h):
        slots = [s.at[h] for s in (stat_w, stat_y, stat_z)]
        return add_over_devices(1 + h, stat_own.at[h], slots)

    def write_targets(h):
        last = stat_own[h, 3]
        earlier = cached_own[3]
        w = half // tail_cut
        for j in range(h * chunks // 2, (h + 1) * chunks // 2):
            cols = slice(j * CHUNK, (j + 1) * CHUNK)
            summed = jnp.zeros((tok, CHUNK), F32)
            for layer in range(4):
                if layer < 3:
                    sums = earlier[8 * layer + j : 8 * layer + j + 1, :]
                    squares = earlier[8 * layer + 4 + j : 8 * layer + 5 + j, :]
                    values = cached_ref[layer, :, cols].astype(F32)
                else:
                    k = (j - h * chunks // 2) * (CHUNK // w)
                    sums = jnp.concatenate([last[k : k + 1], last[k + 1 : k + 2]], axis=1)
                    squares = jnp.concatenate([last[4 + k : 5 + k], last[5 + k : 6 + k]], axis=1)
                    values = layer_out[:, cols]
                mean = sums / total_tokens
                variance = squares / total_tokens - mean * mean
                summed = summed + (values - mean) * lax.rsqrt(variance + 1e-5)
            targets = (summed * 0.25).astype(BF16)
            targets_ref[:, cols] = targets
            if (j + 1) * CHUNK <= window:
                residuals[0, :, cols] = (
                    (prediction_ref[:, cols].astype(F32) - targets.astype(F32)) * scale
                ).astype(BF16)

    send_back(2, 1, 20)
    combine(0)
    sums = add_statistics(0)
    next(sums, None)
    send_back(2, 20, 28)
    next(sums, None)
    send_back(2, 28, 36)
    next(sums, None)
    send_back(2, 36, 44)
    next(sums, None)
    write_targets(0)
    pieces = [slice(k * CHUNK, (k + 1) * CHUNK) for k in range(window // CHUNK)]
    over_x = [
        start_all(
            axes["x"],
            lambda d: residuals.at[0, :, cols],
            lambda d: residuals.at[d, :, cols],
            sem_x.at[k, 0],
            sem_x.at[k, 1],
        )
        for k, cols in enumerate(pieces)
    ]
    send_back(2, 44, n)
    project(3)
    send_back(3, 1, 20)
    wait_all(students_out)
    rows = students.shape[1]
    partial = raised.at[pl.ds(0, rows), pl.ds(0, window)]
    halved = rows // 2
    other = pl.ds(pl.multiple_of((1 - c) * halved, halved), halved)
    kept = pl.ds(pl.multiple_of(c * halved, halved), halved)
    part = halved // ny
    least = part // nz

    def y_rows(d):
        return pl.ds(pl.multiple_of(lax.rem(y + d, ny) * part, part), part)

    def z_rows(d):
        return pl.ds(pl.multiple_of(lax.rem(z + d, nz) * least, least), least)

    over_c, over_y, over_z = [], [], []
    for k, cols in enumerate(pieces):
        for d in range(nx):
            if d:
                over_x[k][d - 1].wait_recv()

            def add(i, _):
                at = pl.ds(pl.multiple_of(i * 128, 128), 128)
                product = jnp.dot(
                    students[d, at, :], residuals[d, :, cols], preferred_element_type=F32
                )
                partial[at, cols] = product if d == 0 else partial[at, cols] + product
                return _

            lax.fori_loop(0, rows // 128, add, 0)
        over_c.append(
            start_all(
                axes["c"],
                lambda d: partial.at[other, cols],
                lambda d: from_c.at[:, cols],
                sem_c.at[k, 0],
                sem_c.at[k, 1],
            )
        )
        send_back(3, (20, 42)[k], (42, n)[k])
    for k, cols in enumerate(pieces):
        wait_all(over_c[k])
        from_c[:, cols] = from_c[:, cols] + partial[kept, cols]
        over_y.append(
            start_all(
                axes["y"],
                lambda d: from_c.at[y_rows(d), cols],
                lambda d: from_y.at[d, :, cols],
                sem_y.at[k, 0],
                sem_y.at[k, 1],
            )
        )
    for k, cols in enumerate(pieces):
        wait_all(over_y[k])
        total = from_c[y_rows(0), cols]
        for d in range(1, ny):
            total = total + from_y[d, :, cols]
        from_y[0, :, cols] = total
        over_z.append(
            start_all(
                axes["z"],
                lambda d: from_y.at[0, z_rows(d), cols],
                lambda d: from_z.at[d, :, cols],
                sem_z.at[k, 0],
                sem_z.at[k, 1],
            )
        )
    combine(1)
    sums = add_statistics(1)
    for _ in range(4):
        next(sums, None)
    write_targets(1)
    for k, cols in enumerate(pieces):
        wait_all(over_z[k])
        total = from_y[0, z_rows(0), cols]
        for d in range(1, nz):
            total = total + from_z[d, :, cols]
        grad_ref[:, cols] = total
        for copy in over_x[k]:
            copy.wait_send()

    for piece in (gate_piece, up_piece, *down_pieces):
        for copy in piece:
            copy.wait_send()
    for copy in (*picks_out, *rings[0], *rings[1]):
        copy.wait_send()
    for j in range(chunks // 2, chunks):
        wait_rows(out, n - 1, slice(j * CHUNK, (j + 1) * CHUNK), sem_back.at[0, j])


def run(total_tokens, gain, router, routes, hidden_in, cached, prediction, student, wg, wu, wd):
    tok, width = hidden_in.shape
    window = prediction.shape[1]
    nx, ny, nz = lax.axis_size("seq"), NY, lax.axis_size("expert") // NY
    rows = width // nx
    hidden_units = wg.shape[1]
    pieces = window // CHUNK
    arrived = router.shape[0] * SLOTS
    chunks = width // CHUNK
    vmem = pl.BlockSpec(memory_space=pltpu.VMEM)
    hbm = pl.BlockSpec(memory_space=pl.ANY)
    dma = pltpu.SemaphoreType.DMA
    early, late = (24, width // 4), (8, width // 8)
    return pl.pallas_call(
        functools.partial(kernel, total_tokens),
        out_shape=(
            jax.ShapeDtypeStruct((tok, width), BF16),
            jax.ShapeDtypeStruct((rows // (2 * ny * nz), window), F32),
        ),
        in_specs=[vmem] * 4 + [hbm] * 6,
        out_specs=(vmem, vmem),
        scratch_shapes=[
            pltpu.VMEM((width, hidden_units), BF16),
            pltpu.VMEM((width, hidden_units), BF16),
            pltpu.VMEM((hidden_units, width), BF16),
            pltpu.VMEM(cached.shape, BF16),
            pltpu.VMEM(prediction.shape, BF16),
            pltpu.VMEM((arrived, tok), BF16),
            pltpu.VMEM((2 * tok, arrived), BF16),
            pltpu.VMEM((nz, tok, width), BF16),
            pltpu.VMEM((nz, arrived // nz, tok), BF16),
            pltpu.VMEM((arrived, width), BF16),
            pltpu.VMEM((arrived, hidden_units), F32),
            pltpu.VMEM((arrived, hidden_units), F32),
            pltpu.VMEM((arrived, hidden_units), BF16),
            pltpu.VMEM((arrived, width), BF16),
            pltpu.VMEM((arrived, width), BF16),
            pltpu.VMEM((tok, width), F32),
            pltpu.VMEM((4, *early), F32),
            pltpu.VMEM((2 * nx - 1, *early), F32),
            pltpu.VMEM((ny - 1, *early), F32),
            pltpu.VMEM((nz - 1, *early), F32),
            pltpu.VMEM((2, 4, *late), F32),
            pltpu.VMEM((2, 2 * nx - 1, *late), F32),
            pltpu.VMEM((2, ny - 1, *late), F32),
            pltpu.VMEM((2, nz - 1, *late), F32),
            pltpu.VMEM((nx, rows, tok), BF16),
            pltpu.VMEM((nx, tok, window), BF16),
            pltpu.VMEM((rows // 2, window), F32),
            pltpu.VMEM((ny, rows // (2 * ny), window), F32),
            pltpu.VMEM((nz, rows // (2 * ny * nz), window), F32),
            dma((6,)),
            dma((2 + chunks, 2, 6)),
            dma((2, 2, nz - 1)),
            dma((2, nz - 1)),
            dma((2,)),
            dma((2, chunks)),
            dma((2, nx - 1)),
            dma((3, 3, 2, 7)),
            dma((pieces, 2, nx - 1)),
            dma((pieces, 2, 1)),
            dma((pieces, 2, ny - 1)),
            dma((pieces, 2, nz - 1)),
        ],
        compiler_params=pltpu.CompilerParams(
            collective_id=1, has_side_effects=True, vmem_limit_bytes=60 * 2**20
        ),
    )(gain, router, routes, hidden_in, cached, prediction, student, wg, wu, wd)


def body(
    hidden_in,
    norm_gain,
    router_weight,
    routes,
    w_gate,
    w_up,
    w_down,
    cached_layers,
    student_hidden,
    prediction,
):
    tok, width = hidden_in.shape
    nx, nz = lax.axis_size("seq"), lax.axis_size("expert") // NY
    total_tokens = tok * lax.axis_size(("expert", "seq", "dp"))
    student = (
        student_hidden.T.reshape(nz, NY, nx, 2, width // (2 * nx * NY * nz), tok)
        .transpose(2, 3, 1, 0, 4, 5)
        .reshape(nx, width // nx, tok)
    )
    return run(
        total_tokens,
        norm_gain[None],
        router_weight.T,
        routes.T,
        hidden_in,
        cached_layers,
        prediction,
        student,
        w_gate[0],
        w_up[0],
        w_down[0],
    )


def solution(mesh):
    tokens = P(("expert", "seq", "dp"), None)
    weights = P(("expert", "dp"), "seq", None)
    return jax.shard_map(
        body,
        mesh=mesh,
        in_specs=(
            tokens,
            P(),
            P(),
            tokens,
            weights,
            weights,
            weights,
            P(None, ("expert", "seq", "dp"), None),
            tokens,
            tokens,
        ),
        out_specs=(tokens, tokens),
        check_vma=False,
    )
```
